256 devices in a mesh: ctx: 4 (over x), exp: 64 (over z, y, core).
Axes of the slice: x: 4, y: 4, z: 8, core: 2. Of those that a mesh axis runs over, the one named last changes fastest.
Arguments:
- moe_input: bfloat16 [8192, 3584], P('exp', 'ctx'), may hold values from -6 to 6
- moe_grad: bfloat16 [8192, 3584], P('exp', 'ctx'), may hold values from -6 to 6
- routes: int32 [8192, 8], P('exp'), may hold values from 0 to 127, all different within a row; in each aligned block of 128 rows (0 to 127, 128 to 255, ...) at most 10 rows name the same one
- gates: float32 [8192, 8], P('exp'), may hold values from 0.05 to 0.5
- w_gate: bfloat16 [128, 3584, 1024], P('exp', 'ctx'), may hold values from -0.09375 to 0.09375
- w_up: bfloat16 [128, 3584, 1024], P('exp', 'ctx'), may hold values from -0.09375 to 0.09375
- w_down: bfloat16 [128, 1024, 3584], P('exp', None, 'ctx'), may hold values from -0.1875 to 0.1875
- queries: bfloat16 [512, 73728], P('ctx', 'exp'), may hold values from -16 to 16
- out_grad: bfloat16 [512, 65536], P('ctx', 'exp'), may hold values from -6 to 6
- positions: int32 [512], P('ctx'), may hold values from 0 to 1023, as said below
- latents: bfloat16 [1024, 576], P('ctx'), may hold values from -6 to 6
Outputs:
- moe_input_grad: bfloat16 [8192, 3584], P('exp', 'ctx')
- query_grad: bfloat16 [512, 73728], P('ctx', 'exp')
- latent_grad: float32 [1024, 576], P(('ctx', 'exp'))
The draws below stay inside these ranges and needn't reach their ends.
Inputs may be any that keep to these rules, and one draw needn't show every extreme that they name: `routes`: each row names 8 different experts; among the 128 rows of one index of exp no expert is named more than 10 times, and in some such block one is named exactly 10 times. Row i lies within the keys of its own context shard, (i // 128) * 256 <= positions[i] < (i // 128 + 1) * 256; the first row of each shard sits at the shard's first key and the last row at its last key.
All inputs are finite; a program needn't handle non-finite values.
Results may differ from the reference program's by a relative error of at most 0.018.
Values may be sent and summed in bfloat16 or wider, within the bound.
A program may use at most 128 MiB of HBM per device.

```python
import math
import jax
import jax.numpy as jnp
import numpy as np
from jax import lax

D = 3584
HID = 1024
TOP = 8
TOK_DEV = 128
LAT = 576
VAL = 512
QROWS = 128
KEY_DEV = 256
EXPERTS = 128
CAP = 10
TOKENS = 8192
DQ = 896
HEADS = 128
QALL = 512
KEYS = 1024
N_EXP = 64


def latent_table(key):
    base = jax.random.fold_in(key, 11)
    table = jax.random.truncated_normal(base, -4.0, 4.0, (KEYS, LAT), jnp.float32)
    return table


def draw_latents(key, part):
    return latent_table(key).astype(jnp.bfloat16)


def draw_queries(key, part):
    base = jax.random.fold_in(key, 23)
    values = jax.random.truncated_normal(base, -4.0, 4.0, (QALL, HEADS * LAT), jnp.float32)
    return values.astype(jnp.bfloat16)


def draw_positions(key, part):
    row_ids = jnp.arange(QALL, dtype=jnp.int32)
    shard = row_ids // QROWS
    inner = row_ids % QROWS
    offset = jax.random.randint(jax.random.fold_in(key, 31), (QALL,), 0, KEY_DEV, dtype=jnp.int32)
    offset = jnp.where(inner == 0, 0, offset)
    offset = jnp.where(inner == QROWS - 1, KEY_DEV - 1, offset)
    return (shard * KEY_DEV + offset).astype(jnp.int32)


def block_scale(stream_key, shape, pieces, smallest, largest):
    level, own = 1.0, jax.random.fold_in(stream_key, 6)
    for axis_at, blocks in pieces:
        draws = jnp.exp(jax.random.uniform(jax.random.fold_in(own, axis_at), (blocks,), jnp.float32, smallest / len(pieces), largest / len(pieces)))
        level = level * jnp.repeat(draws, shape[axis_at] // blocks).reshape([-1 if axis == axis_at else 1 for axis in range(len(shape))])
    return level


def routed_block(rng, own, number, rows, amount, top, reach, skew):
    sequence = jax.random.permutation(rng, amount)
    crowded, usual = shares(amount, rows * top, reach, skew, True), shares(amount, rows * top, reach, skew, False)
    places = jnp.arange(amount)

    def named(tallies, turn):
        used = int((tallies > 0).sum())
        fixed = max(1, used // 4)
        moved = fixed + (places - fixed + turn * (used - fixed)) % max(1, amount - fixed)
        return jnp.zeros((amount,), jnp.int32).at[sequence[jnp.where(places < fixed, places, moved)]].set(jnp.asarray(tallies, jnp.int32))

    tallies = jnp.where(number % 4 == 0, named(crowded, number // 4), named(usual, number - number // 4 - 1))
    mixed = jax.random.permutation(jax.random.fold_in(own, 3), amount)
    source_of, sink = mixed[0:amount // 2 * 2:2], mixed[1:amount // 2 * 2:2]
    margin = jnp.minimum(tallies[source_of] - 1, reach - tallies[sink]) // 2
    margin = jnp.where((source_of == sequence[0]) | (sink == sequence[0]) | (tallies[sink] == 0), 0, jnp.maximum(margin, 0))
    moved = jax.random.randint(jax.random.fold_in(own, 4), (amount // 2,), 0, 1 << 20) % (margin + 1)
    tallies = tallies.at[source_of].add(-moved).at[sink].add(moved)
    members = jnp.searchsorted(jnp.cumsum(tallies), jnp.arange(rows * top), side="right").astype(jnp.int32)
    table = members.reshape(top, rows).T
    table = table[jax.random.permutation(jax.random.fold_in(own, 1), rows)]
    turn = jax.random.randint(jax.random.fold_in(own, 2), (rows, 1), 0, top)
    return jnp.take_along_axis(table, (jnp.arange(top)[None, :] + turn) % top, axis=1)


def shares(number_of, total, limit, skew, full):
    weights = [(1 << 20) // math.isqrt(rank ** skew) + 1 for rank in range(1, number_of + 1)]
    largest = limit if full else min(limit, max(-(-total // number_of), total * weights[0] // sum(weights)))
    least = 1 if total - largest >= number_of - 1 else 0
    given, rest = [largest] + [least] * (number_of - 1), total - largest - least * (number_of - 1)
    while rest > 0:
        candidates = [i for i in range(1, number_of) if given[i] < largest] or [i for i in range(1, number_of) if given[i] < limit]
        pool, remaining = sum([weights[i] for i in candidates]), rest
        for i in candidates:
            addition = min(limit - given[i], max(1, remaining * weights[i] // pool), rest)
            given[i] = given[i] + addition
            rest = rest - addition
    return np.array(given)


def scatter_about(rng, extent, spread, bound, pieces=(), kind=jnp.bfloat16):
    gain = block_scale(rng, extent, pieces, -0.22, 0.18) if pieces else 1.0
    array = jax.random.normal(rng, extent, jnp.float32) * spread * gain
    return jnp.minimum(jnp.maximum(array, -bound), bound).astype(kind)


def setup_inputs(seed: int = 0) -> dict:
    key_of = jax.random.split(jax.random.key(seed), 12)
    moe_input = scatter_about(key_of[0], (TOKENS, D), 1.0, 6.0, ((0, 64), (1, 4)))
    moe_grad = scatter_about(key_of[1], (TOKENS, D), 1.0, 6.0, ((0, 64), (1, 4)))
    routes_keys = jax.random.split(jax.random.fold_in(key_of[2], 1), TOKENS // TOK_DEV)
    routes_turns = jax.random.permutation(jax.random.fold_in(key_of[2], 3), TOKENS // TOK_DEV)
    routes = jax.vmap(lambda own, number: routed_block(jax.random.fold_in(key_of[2], 2), own, number, TOK_DEV, EXPERTS, TOP, CAP, 2))(routes_keys, routes_turns).reshape((TOKENS, TOP))
    gates = jnp.clip(0.05 + 0.45 * jax.random.uniform(key_of[3], (TOKENS, TOP), jnp.float32) ** block_scale(key_of[3], (TOKENS, TOP), ((0, 64),), -0.2, 0.2), 0.05, 0.5)
    w_gate = scatter_about(key_of[4], (EXPERTS, D, HID), D ** -0.5, 0.09375, ((0, 64), (1, 4)))
    w_up = scatter_about(key_of[5], (EXPERTS, D, HID), D ** -0.5, 0.09375, ((0, 64), (1, 4)))
    w_down = scatter_about(key_of[6], (EXPERTS, HID, D), HID ** -0.5, 0.1875, ((0, 64), (2, 4)))
    queries = draw_queries(jax.random.fold_in(key_of[11], 71), 0)
    out_grad = scatter_about(key_of[8], (QALL, HEADS * VAL), 1.0, 6.0, ((0, 4), (1, 64)))
    positions = draw_positions(jax.random.fold_in(key_of[11], 71), 0)
    latents = draw_latents(jax.random.fold_in(key_of[11], 71), 0)
    return dict(moe_input=moe_input, moe_grad=moe_grad, routes=routes, gates=gates, w_gate=w_gate, w_up=w_up, w_down=w_down, queries=queries, out_grad=out_grad, positions=positions, latents=latents)


SCORE_SCALE = 192.0 ** -0.5
MASKED = -1.0e30


def swiglu_back(gate_pre, up_pre, hidden_grad):
    sigma = jax.nn.sigmoid(gate_pre)
    gate_back = hidden_grad * up_pre * sigma * (1.0 + gate_pre * (1.0 - sigma))
    up_back = hidden_grad * gate_pre * sigma
    return gate_back.astype(jnp.bfloat16), up_back.astype(jnp.bfloat16)


def rounded_blocks(left, right):
    partial_sums = jnp.einsum("mcd,cdh->mch", left, right)
    lowered = lax.optimization_barrier(partial_sums.astype(jnp.bfloat16))
    return jnp.sum(lowered.astype(jnp.float32), axis=1)


def expert_ranks(block_routes):
    onehot = (block_routes[:, None] == jnp.arange(EXPERTS, dtype=jnp.int32)[None, :]).astype(jnp.int32)
    before = jnp.cumsum(onehot, axis=0) - onehot
    return jnp.sum(before * onehot, axis=1).astype(jnp.int32)


def expert_part(moe_input, moe_grad, routes, gates, w_gate, w_up, w_down):
    per_block = TOK_DEV * TOP
    block_routes = routes.reshape(N_EXP, per_block).astype(jnp.int32)
    slots = lax.map(expert_ranks, block_routes)
    column = (jnp.arange(N_EXP, dtype=jnp.int32)[:, None] * CAP + slots).astype(jnp.int32)
    route_ids = jnp.arange(TOKENS * TOP, dtype=jnp.int32).reshape(N_EXP, per_block)
    table = jnp.full((EXPERTS, N_EXP * CAP), -1, jnp.int32).at[block_routes, column].set(route_ids)
    flat_gates = gates.reshape(-1)
    blocks = D // DQ

    def expert_step(carry, packed):
        row_table, gate_weight, up_weight, down_weight = packed
        valid = row_table >= 0
        route_index = jnp.where(valid, row_table, 0).astype(jnp.int32)
        token_index = (route_index // TOP).astype(jnp.int32)
        rows_in = moe_input[token_index].astype(jnp.float32).reshape(-1, blocks, DQ)
        rows_grad = moe_grad[token_index].astype(jnp.float32).reshape(-1, blocks, DQ)
        gate_pre = rounded_blocks(rows_in, gate_weight.astype(jnp.float32).reshape(blocks, DQ, HID))
        up_pre = rounded_blocks(rows_in, up_weight.astype(jnp.float32).reshape(blocks, DQ, HID))
        down_blocks = jnp.transpose(down_weight.astype(jnp.float32).reshape(HID, blocks, DQ), (1, 2, 0))
        hidden_grad = rounded_blocks(rows_grad, down_blocks)
        gate_back, up_back = swiglu_back(gate_pre, up_pre, hidden_grad)
        route_grad = jnp.dot(gate_back, gate_weight.T, preferred_element_type=jnp.float32)
        route_grad = route_grad + jnp.dot(up_back, up_weight.T, preferred_element_type=jnp.float32)
        lowered = lax.optimization_barrier(route_grad.astype(jnp.bfloat16)).astype(jnp.float32)
        scaled = jnp.where(valid[:, None], flat_gates[route_index][:, None] * lowered, 0.0)
        return carry.at[token_index].add(scaled), None

    total, _ = lax.scan(expert_step, jnp.zeros((TOKENS, D), jnp.float32), (table, w_gate, w_up, w_down))
    return total.astype(jnp.bfloat16)


def attention_part(queries, out_grad, positions, latents):
    query_heads = jnp.transpose(queries.reshape(QALL, HEADS, LAT), (1, 0, 2))
    grad_heads = jnp.transpose(out_grad.reshape(QALL, HEADS, VAL), (1, 0, 2))
    visible = jnp.arange(KEYS, dtype=jnp.int32)[None, :] <= positions[:, None]
    values = latents[:, :VAL]

    def head_step(carry, packed):
        query_one, grad_one = packed
        scores = jnp.dot(query_one, latents.T, preferred_element_type=jnp.float32) * SCORE_SCALE
        scores = jnp.where(visible, scores, MASKED)
        peak = jnp.max(scores, axis=1, keepdims=True)
        raw = jnp.where(visible, jnp.exp(scores - peak), 0.0)
        attend = raw / jnp.sum(raw, axis=1, keepdims=True)
        value_dot = jnp.dot(grad_one, values.T, preferred_element_type=jnp.float32)
        row_dot = jnp.sum(attend * value_dot, axis=1, keepdims=True)
        score_grad = (attend * (value_dot - row_dot)).astype(jnp.bfloat16)
        query_grad = jnp.dot(score_grad, latents, preferred_element_type=jnp.float32) * SCORE_SCALE
        key_grad = jnp.dot(score_grad.T, query_one, preferred_element_type=jnp.float32) * SCORE_SCALE
        value_grad = jnp.dot(attend.astype(jnp.bfloat16).T, grad_one, preferred_element_type=jnp.float32)
        carry = carry + key_grad + jnp.pad(value_grad, ((0, 0), (0, LAT - VAL)))
        return carry, query_grad.astype(jnp.bfloat16)

    latent_grad, query_grads = lax.scan(head_step, jnp.zeros((KEYS, LAT), jnp.float32), (query_heads, grad_heads))
    query_grad = jnp.transpose(query_grads, (1, 0, 2)).reshape(QALL, HEADS * LAT)
    return query_grad, latent_grad


def reference(moe_input, moe_grad, routes, gates, w_gate, w_up, w_down, queries, out_grad, positions, latents):
    moe_input_grad = expert_part(moe_input, moe_grad, routes, gates, w_gate, w_up, w_down)
    query_grad, latent_grad = attention_part(queries, out_grad, positions, latents)
    return (moe_input_grad, query_grad, latent_grad)
```

```python
import jax
import jax.numpy as jnp
from jax import lax
from jax.experimental import pallas as pl
from jax.experimental.pallas import tpu as pltpu
from jax.sharding import PartitionSpec as P

SCORE_SCALE = 192.0 ** (-0.5)
MASKED = -1e30
MESH = pl.DeviceIdType.MESH
BF = jnp.bfloat16
F32 = jnp.float32

NX, NZ, NY, NC = 4, 8, 4, 2
NQ = NY * NC
TOK = 128
WID = 896
HID = 1024
CAP = 10
SLOTS = NZ * CAP
LAT = 576
VAL = 512
HEADS = 2
KEY_DEV = 256
KEYS = NX * KEY_DEV

N_ZAG = 16
N_META = 8
N_LAT = 4
N_PLANE = 32
N_BACK = 16
N_RS = 24
N_AG = 16
N_ZRS = 8
N_LG = 1 + 8 + 4 + 4

OFF_ZAG = 0
OFF_META = OFF_ZAG + N_ZAG
OFF_LAT = OFF_META + N_META
OFF_PLANE = OFF_LAT + N_LAT
OFF_BACK = OFF_PLANE + N_PLANE
OFF_RS = OFF_BACK + N_BACK
OFF_AG = OFF_RS + N_RS
OFF_ZRS = OFF_AG + N_AG
OFF_LG = OFF_ZRS + N_ZRS
N_SEM = OFF_LG + N_LG


def nn(a, b):
    return lax.dot_general(a, b, (((1,), (0,)), ((), ())), preferred_element_type=F32)


def nt(a, b):
    return lax.dot_general(a, b, (((1,), (1,)), ((), ())), preferred_element_type=F32)


def tn(a, b):
    return lax.dot_general(a, b, (((0,), (0,)), ((), ())), preferred_element_type=F32)


def body(
    in_hbm, grad_hbm, meta_hbm, wg_hbm, wu_hbm, wd_hbm, q_hbm, og_hbm, pos_ref, lat_hbm,
    out_ref, qg_ref, lg_ref,
    tok, meta, wg, wu, wd, qv, ogv, latraw, lat, rank_s, gate_s, pick, ysend, yrecv,
    part, rs_mid, rs_in, bk, rsend, rrecv, zsend_v, zhalf, zrecv,
    lacc, lout, lc_in, lz_out, lz_in, lx_out, lx_in, ly_out, ly_in,
    ssem, rsem, lsem,
):
    x = lax.axis_index("ctx")
    e_id = lax.axis_index("exp")
    z = e_id // NQ
    q = e_id % NQ
    y = q // NC
    c = q % NC

    def dev(xx, zz, qq):
        return (xx, zz * NQ + qq)

    def zdev(d):
        return dev(x, (z + d + NZ) % NZ, q)

    def xdev(d):
        return dev((x + d + NX) % NX, z, q)

    def plane(dy, dc):
        return ((y + dy + NY) % NY) * NC + (c + dc) % NC

    sends = []

    def copy(src, dst, idx, to):
        return pltpu.make_async_remote_copy(
            src_ref=src, dst_ref=dst, send_sem=ssem.at[idx], recv_sem=rsem.at[idx],
            device_id=to, device_id_type=MESH,
        )

    def send(src, dst, idx, to):
        op = copy(src, dst, idx, to)
        op.start()
        sends.append(op)

    def arrived(dst, idx, frm):
        copy(dst, dst, idx, frm).wait_recv()

    loads = []

    def load(src, dst):
        op = pltpu.make_async_copy(src, dst, lsem.at[len(loads)])
        op.start()
        loads.append(op)
        return op

    ld_in = load(in_hbm, tok.at[0, z])
    ld_meta = load(meta_hbm, meta.at[z])
    ld_lat = load(lat_hbm, latraw)
    ld_grad = load(grad_hbm, tok.at[1, z])
    ld_q = load(q_hbm, qv)
    ld_og = load(og_hbm, ogv)
    ld_wg = load(wg_hbm, wg)
    ld_wu = load(wu_hbm, wu)
    ld_wd = load(wd_hbm, wd)

    barrier = pltpu.get_barrier_semaphore()
    peers = [zdev(d) for d in range(1, NZ)]
    peers += [dev(x, z, plane(j // NC, j % NC)) for j in range(1, NQ)]
    peers += [xdev(d) for d in range(1, NX)]
    for peer in peers:
        pl.semaphore_signal(barrier, inc=1, device_id=peer, device_id_type=MESH)
    pl.semaphore_wait(barrier, len(peers))

    def zidx(a, way, step):
        return OFF_ZAG + (a * 2 + way) * 4 + step

    half = (pl.ds(0, TOK // 2), pl.ds(TOK // 2, TOK // 2))

    def zblock(a, way, step):
        b = (z - step + NZ) % NZ if way == 0 else (z + step) % NZ
        return tok.at[a, b] if step < 4 else tok.at[a, b, half[way]]

    def zsend(a, step):
        for way in (0, 1):
            b = (z - step + NZ) % NZ if way == 0 else (z + step) % NZ
            blk = tok.at[a, b] if step < 3 else tok.at[a, b, half[way]]
            send(blk, blk, zidx(a, way, step), zdev(1 if way == 0 else -1))

    def zarrive(a, step):
        for way in (0, 1):
            arrived(zblock(a, way, step), zidx(a, way, step - 1), zdev(-1 if way == 0 else 1))

    ld_in.wait()
    zsend(0, 0)
    ld_meta.wait()
    for d in range(1, NZ):
        send(meta.at[z], meta.at[z], OFF_META + d, zdev(d))

    ld_lat.wait()
    new = lax.broadcasted_iota(jnp.int32, (KEY_DEV, KEY_DEV), 0)
    old = lax.broadcasted_iota(jnp.int32, (KEY_DEV, KEY_DEV), 1)
    src = ((new // 16) % 8) * 32 + ((new // 4) % 4) * 8 + (new // 128) * 4 + new % 4
    shuffle = jnp.where(src == old, 1.0, 0.0).astype(BF)
    lat[x] = nn(shuffle, latraw[...]).astype(BF)
    for d in range(1, NX):
        send(lat.at[x], lat.at[x], OFF_LAT + d, xdev(d))

    for d in range(1, NZ):
        b = (z - d + NZ) % NZ
        arrived(meta.at[b], OFF_META + d, dev(x, b, q))
    tri = jnp.where(
        lax.broadcasted_iota(jnp.int32, (TOK, TOK), 0) < lax.broadcasted_iota(jnp.int32, (TOK, TOK), 1),
        1.0, 0.0,
    ).astype(BF)
    names = (lax.broadcasted_iota(jnp.int32, (2 * NQ, TOK), 0) + z * (2 * NQ)).astype(F32)
    for b in range(NZ):
        member = jnp.zeros((2 * NQ, TOK), F32)
        gate = jnp.zeros((2 * NQ, TOK), F32)
        for k in range(8):
            hit = meta[b, k : k + 1, :] == names
            member = jnp.where(hit, 1.0, member)
            gate = jnp.where(hit, meta[b, 8 + k : 9 + k, :], gate)
        rank = nn(member.astype(BF), tri)
        rank_s[b] = jnp.where(member > 0.0, rank, -1.0)
        gate_s[b] = gate

    def slot_value(b):
        row = lax.broadcasted_iota(jnp.int32, (SLOTS, TOK), 0)
        return jnp.where(row % NZ == b, row // NZ, -5).astype(F32)

    def build(weighted):
        for b in range(NZ):
            value = slot_value(b)

            def one(i, carry):
                row = rank_s[b, pl.ds(i, 1), :]
                if weighted:
                    cell = jnp.where(row == value, gate_s[b, pl.ds(i, 1), :], 0.0)
                else:
                    cell = jnp.where(row == value, 1.0, 0.0)
                pick[i, :, b * TOK : (b + 1) * TOK] = cell.astype(BF)
                return carry

            lax.fori_loop(0, 2 * NQ, one, 0)

    zarrive(0, 1)
    zsend(0, 1)

    ld_q.wait()
    ld_og.wait()
    for d in range(1, NX):
        arrived(lat.at[(x - d + NX) % NX], OFF_LAT + d, xdev(-d))

    col = lax.broadcasted_iota(jnp.int32, (TOK, KEYS), 1)
    key_pos = (
        (col // 256) * 256 + ((col // 16) % 8) * 32 + ((col // 4) % 4) * 8 + ((col // 128) % 2) * 4 + col % 4
    )

    def attention(h):
        keys = lat[...].reshape(KEYS, LAT)
        visible = key_pos <= pos_ref[...]
        qh = qv[h]
        gh = ogv[h]
        score = jnp.where(visible, nt(qh, keys) * SCORE_SCALE, MASKED)
        peak = jnp.max(score, axis=1, keepdims=True)
        raw = jnp.where(visible, jnp.exp(score - peak), 0.0)
        attend = raw / jnp.sum(raw, axis=1, keepdims=True)
        dots = nt(gh, keys[:, :VAL])
        row_dot = jnp.sum(attend * dots, axis=1, keepdims=True)
        grad = (attend * (dots - row_dot)).astype(BF)
        low = attend.astype(BF)
        qg_ref[h] = (nn(grad, keys) * SCORE_SCALE).astype(BF)
        key_part = tn(grad, qh) * SCORE_SCALE
        val_part = tn(low, gh)
        if h == 0:
            lacc[...] = key_part
        else:
            lacc[...] += key_part
        lacc[:, :VAL] += val_part

    attention(0)
    zarrive(0, 2)
    zsend(0, 2)
    attention(1)
    lout[...] = lacc[...].astype(BF).reshape(NX, NC, 128, LAT)
    sib = plane(0, 1)
    send(lout.at[:, 1 - c], lc_in, OFF_LG, dev(x, z, sib))
    zarrive(0, 3)
    zsend(0, 3)
    ld_grad.wait()
    zsend(1, 0)

    build(False)
    zarrive(0, 4)

    def pidx(a, e, j):
        return OFF_PLANE + (a * 2 + e) * NQ + j

    ORDER = (4, 5, 2, 3, 6, 7, 1)

    def pack(a):
        toks = tok[a].reshape(NZ * TOK, WID)

        def rows_for(qq):
            return nn(pick[pl.ds(qq * 2, 2)].reshape(2 * SLOTS, NZ * TOK), toks).astype(BF)

        for j in ORDER:
            qq = plane(j // NC, j % NC)
            ysend[a, qq] = rows_for(qq).reshape(2, SLOTS, WID)
            send(ysend.at[a, qq, 0], yrecv.at[a, 0, q], pidx(a, 0, j), dev(x, z, qq))
        own = rows_for(q).reshape(2, SLOTS, WID)
        yrecv[a, 0, q] = own[0]
        yrecv[a, 1, q] = own[1]
        for j in ORDER:
            qq = plane(j // NC, j % NC)
            send(ysend.at[a, qq, 1], yrecv.at[a, 1, q], pidx(a, 1, j), dev(x, z, qq))

    def rows_arrive(a, e):
        for j in range(1, NQ):
            frm = plane(-(j // NC), j % NC)
            arrived(yrecv.at[a, e, frm], pidx(a, e, j), dev(x, z, frm))

    pack(0)
    zarrive(1, 1)
    zsend(1, 1)

    arrived(lc_in, OFF_LG, dev(x, z, sib))
    mine = lacc[...].reshape(NX, NC, 128, LAT)
    summed = jnp.where(c == 0, mine[:, 0], mine[:, 1]) + lc_in[...].astype(F32)
    lacc[pl.ds(0, NX * 128)] = summed.reshape(NX * 128, LAT)
    lz_out[...] = summed.astype(BF).reshape(NX, NZ, 16, LAT)
    for d in range(1, NZ):
        send(lz_out.at[:, (z + d) % NZ], lz_in.at[d], OFF_LG + d, zdev(d))

    zarrive(1, 2)
    zsend(1, 2)

    ld_wg.wait()
    ld_wu.wait()
    ld_wd.wait()

    k_opp, k_right, k_left = (x + 2) % NX, (x + 1) % NX, (x + 3) % NX
    right, left = xdev(1), xdev(-1)
    top, bottom = pl.ds(0, SLOTS), pl.ds(SLOTS, SLOTS)

    def partial(e, name, k):
        a, w = {"gate": (0, wg), "up": (0, wu), "down": (1, wd)}[name]
        rows = yrecv[a, e, pl.ds(k * 2, 2)].reshape(2 * SLOTS, WID)
        return nt(rows, w[e]) if name == "down" else nn(rows, w[e])

    UNITS = ((0, 2, ("gate", "up")), (2, 1, ("down",)))

    def ridx(e, u, n):
        return OFF_RS + (e * 2 + u) * 6 + n

    def store_part(e, u, k):
        first, _, names_ = UNITS[u]
        for i, name in enumerate(names_):
            part[e, k, first + i] = partial(e, name, k).astype(BF)

    def reduce_first(e, u):
        first, n, _ = UNITS[u]
        rng = pl.ds(first, n)
        store_part(e, u, k_opp)
        send(part.at[e, k_opp, rng, top], rs_mid.at[0, e, rng], ridx(e, u, 0), right)
        send(part.at[e, k_opp, rng, bottom], rs_mid.at[1, e, rng], ridx(e, u, 1), left)
        store_part(e, u, k_right)
        send(part.at[e, k_right, rng, bottom], rs_in.at[0, e, rng, bottom], ridx(e, u, 2), right)
        store_part(e, u, k_left)
        send(part.at[e, k_left, rng, top], rs_in.at[1, e, rng, top], ridx(e, u, 3), left)

    def reduce_second(e, u):
        first, n, _ = UNITS[u]
        rng = pl.ds(first, n)
        arrived(rs_mid.at[0, e, rng], ridx(e, u, 0), left)
        got = rs_mid[0, e, rng].astype(F32) + part[e, k_right, rng, top].astype(F32)
        part[e, k_right, rng, top] = got.astype(BF)
        send(part.at[e, k_right, rng, top], rs_in.at[0, e, rng, top], ridx(e, u, 4), right)
        arrived(rs_mid.at[1, e, rng], ridx(e, u, 1), right)
        got = rs_mid[1, e, rng].astype(F32) + part[e, k_left, rng, bottom].astype(F32)
        part[e, k_left, rng, bottom] = got.astype(BF)
        send(part.at[e, k_left, rng, bottom], rs_in.at[1, e, rng, bottom], ridx(e, u, 5), left)
        store_part(e, u, x)

    def reduce_last(e):
        for u in (0, 1):
            first, n, _ = UNITS[u]
            rng = pl.ds(first, n)
            arrived(rs_in.at[0, e, rng, bottom], ridx(e, u, 2), left)
            arrived(rs_in.at[1, e, rng, top], ridx(e, u, 3), right)
            arrived(rs_in.at[0, e, rng, top], ridx(e, u, 4), left)
            arrived(rs_in.at[1, e, rng, bottom], ridx(e, u, 5), right)

    def total(e, i, rows):
        return (
            part[e, x, i, rows].astype(F32)
            + rs_in[0, e, i, rows].astype(F32)
            + rs_in[1, e, i, rows].astype(F32)
        )

    def aidx(e, way, n):
        return OFF_AG + (e * 2 + way) * 3 + n

    def swiglu_back(e):
        both = pl.ds(0, 2)
        for rows in (top, bottom):
            gate_pre, up_pre, hidden = (total(e, i, rows) for i in range(3))
            sigma = jax.nn.sigmoid(gate_pre)
            bk[e, x, 0, rows] = (hidden * up_pre * sigma * (1.0 + gate_pre * (1.0 - sigma))).astype(BF)
            bk[e, x, 1, rows] = (hidden * gate_pre * sigma).astype(BF)
        t, b = bk.at[e, x, both, top], bk.at[e, x, both, bottom]
        send(t, t, aidx(e, 0, 0), right)
        send(b, b, aidx(e, 1, 0), left)
        send(b, b, aidx(e, 0, 1), right)
        send(t, t, aidx(e, 1, 1), left)

    def gather_forward(e):
        both = pl.ds(0, 2)
        t = bk.at[e, k_left, both, top]
        arrived(t, aidx(e, 0, 0), left)
        send(t, t, aidx(e, 0, 2), right)
        b = bk.at[e, k_right, both, bottom]
        arrived(b, aidx(e, 1, 0), right)
        send(b, b, aidx(e, 1, 2), left)

    def gather_near(e):
        both = pl.ds(0, 2)
        arrived(bk.at[e, k_left, both, bottom], aidx(e, 0, 1), left)
        arrived(bk.at[e, k_right, both, top], aidx(e, 1, 1), right)

    def gather_far(e):
        both = pl.ds(0, 2)
        arrived(bk.at[e, k_opp, both, top], aidx(e, 0, 2), left)
        arrived(bk.at[e, k_opp, both, bottom], aidx(e, 1, 2), right)

    def bidx(e, j):
        return OFF_BACK + e * NQ + j

    def route(e, k):
        rows = nt(bk[e, k, 0], wg[e]) + nt(bk[e, k, 1], wu[e])
        rsend[e, pl.ds(k * 2, 2)] = rows.astype(BF).reshape(2, SLOTS, WID)
        for cc in range(NC):
            qq = k * NC + cc
            j = ((k - y + NY) % NY) * NC + (cc + c) % NC

            @pl.when(j != 0)
            def _():
                copy(rsend.at[e, qq], rrecv.at[q, e], bidx(e, j), dev(x, z, qq)).start()

            @pl.when(j == 0)
            def _():
                rrecv[q, e] = rsend[e, qq]

    rows_arrive(0, 0)
    reduce_first(0, 0)
    zarrive(1, 3)
    zsend(1, 3)
    reduce_second(0, 0)
    zarrive(1, 4)
    pack(1)
    rows_arrive(0, 1)
    reduce_first(1, 0)
    reduce_second(1, 0)
    build(True)

    zsum = lacc[pl.ds(0, NX * 128)].reshape(NX, NZ, 16, LAT)
    zown = jnp.where(z == 0, zsum[:, 0], 0.0)
    for b in range(1, NZ):
        zown = zown + jnp.where(z == b, zsum[:, b], 0.0)
    for d in range(1, NZ):
        arrived(lz_in.at[d], OFF_LG + d, zdev(-d))
        zown = zown + lz_in[d].astype(F32)
    lx_out[...] = zown
    for d in range(1, NX):
        send(lx_out.at[(x + d) % NX], lx_in.at[d], OFF_LG + 8 + d, xdev(d))

    rows_arrive(1, 0)
    reduce_first(0, 1)
    reduce_second(0, 1)
    rows_arrive(1, 1)
    reduce_first(1, 1)
    reduce_last(0)
    swiglu_back(0)
    reduce_second(1, 1)

    xsum = lx_out[x]
    for d in range(1, NX):
        arrived(lx_in.at[d], OFF_LG + 8 + d, xdev(-d))
        xsum = xsum + lx_in[d]
    ly_out[...] = xsum
    for d in range(1, NY):
        send(ly_out, ly_in.at[d], OFF_LG + 12 + d, dev(x, z, plane(d, 0)))

    gather_forward(0)
    route(0, x)
    reduce_last(1)
    swiglu_back(1)
    gather_near(0)
    route(0, k_left)
    route(0, k_right)
    gather_far(0)
    route(0, k_opp)
    gather_forward(1)
    route(1, x)
    gather_near(1)
    route(1, k_left)
    route(1, k_right)

    ysum = ly_out[...]
    for d in range(1, NY):
        arrived(ly_in.at[d], OFF_LG + 12 + d, dev(x, z, plane(-d, 0)))
        ysum = ysum + ly_in[d]
    pick4 = jnp.where(y == 0, ysum[0:4], 0.0)
    for b in range(1, NY):
        pick4 = pick4 + jnp.where(y == b, ysum[4 * b : 4 * b + 4], 0.0)
    lg_ref[...] = pick4

    gather_far(1)
    route(1, k_opp)

    for e in (0, 1):
        for j in range(1, NQ):
            frm = plane(-(j // NC), j % NC)
            arrived(rrecv.at[frm, e], bidx(e, j), dev(x, z, frm))

    def tokens(b):
        cols = pl.ds(pl.multiple_of(b * TOK, TOK), TOK)
        return tn(
            pick[:, :, cols].reshape(2 * NQ * SLOTS, TOK), rrecv[...].reshape(2 * NQ * SLOTS, WID)
        )

    def widx(way, step):
        return OFF_ZRS + way * 4 + step

    far = tokens((z + 4) % NZ).astype(BF)
    zhalf[0] = far[: TOK // 2]
    zhalf[1] = far[TOK // 2 :]
    for way in (0, 1):
        to = zdev(1 if way == 0 else -1)
        send(zhalf.at[way], zrecv.at[way, 0, half[way]], widx(way, 0), to)
    for step in (1, 2, 3):
        for way in (0, 1):
            b = (z + 4 - step) % NZ if way == 0 else (z + 4 + step) % NZ
            to = zdev(1 if way == 0 else -1)
            frm = zdev(-1 if way == 0 else 1)
            acc = tokens(b)
            if step == 1:
                arrived(zrecv.at[way, 0, half[way]], widx(way, 0), frm)
                got = zrecv[way, 0, half[way]].astype(F32)
                lo, hi = acc[: TOK // 2], acc[TOK // 2 :]
                if way == 0:
                    lo = lo + got
                else:
                    hi = hi + got
                acc = jnp.concatenate([lo, hi], axis=0)
            else:
                arrived(zrecv.at[way, step - 1], widx(way, step - 1), frm)
                acc = acc + zrecv[way, step - 1].astype(F32)
            zsend_v[way, step - 1] = acc.astype(BF)
            send(zsend_v.at[way, step - 1], zrecv.at[way, step], widx(way, step), to)
    final = tokens(z)
    for way in (0, 1):
        frm = zdev(-1 if way == 0 else 1)
        arrived(zrecv.at[way, 3], widx(way, 3), frm)
        final = final + zrecv[way, 3].astype(F32)
    out_ref[...] = final.astype(BF)

    for op in sends:
        op.wait_send()
    for e in (0, 1):
        for j in range(1, NQ):
            copy(rsend.at[e, 0], rrecv.at[0, e], bidx(e, j), dev(x, z, plane(j // NC, j % NC))).wait_send()


def per_device(
    moe_input, moe_grad, routes, gates, w_gate, w_up, w_down, queries, out_grad, positions, latents
):
    meta = jnp.concatenate([routes.T.astype(F32), gates.T], axis=0)
    q_heads = queries.reshape(TOK, HEADS, LAT).transpose(1, 0, 2)
    g_heads = out_grad.reshape(TOK, HEADS, VAL).transpose(1, 0, 2)
    anywhere = pl.BlockSpec(memory_space=pl.ANY)
    vmem = pl.BlockSpec(memory_space=pltpu.VMEM)
    scratch = [
        pltpu.VMEM((2, NZ, TOK, WID), BF),
        pltpu.VMEM((NZ, 16, TOK), F32),
        pltpu.VMEM((2, WID, HID), BF),
        pltpu.VMEM((2, WID, HID), BF),
        pltpu.VMEM((2, HID, WID), BF),
        pltpu.VMEM((HEADS, TOK, LAT), BF),
        pltpu.VMEM((HEADS, TOK, VAL), BF),
        pltpu.VMEM((KEY_DEV, LAT), BF),
        pltpu.VMEM((NX, KEY_DEV, LAT), BF),
        pltpu.VMEM((NZ, 2 * NQ, TOK), F32),
        pltpu.VMEM((NZ, 2 * NQ, TOK), F32),
        pltpu.VMEM((2 * NQ, SLOTS, NZ * TOK), BF),
        pltpu.VMEM((2, NQ, 2, SLOTS, WID), BF),
        pltpu.VMEM((2, 2, NQ, SLOTS, WID), BF),
        pltpu.VMEM((2, NX, 3, 2 * SLOTS, HID), BF),
        pltpu.VMEM((2, 2, 3, SLOTS, HID), BF),
        pltpu.VMEM((2, 2, 3, 2 * SLOTS, HID), BF),
        pltpu.VMEM((2, NX, 2, 2 * SLOTS, HID), BF),
        pltpu.VMEM((2, NQ, SLOTS, WID), BF),
        pltpu.VMEM((NQ, 2, SLOTS, WID), BF),
        pltpu.VMEM((2, 3, TOK, WID), BF),
        pltpu.VMEM((2, TOK // 2, WID), BF),
        pltpu.VMEM((2, 4, TOK, WID), BF),
        pltpu.VMEM((KEYS, LAT), F32),
        pltpu.VMEM((NX, NC, 128, LAT), BF),
        pltpu.VMEM((NX, 128, LAT), BF),
        pltpu.VMEM((NX, NZ, 16, LAT), BF),
        pltpu.VMEM((NZ, NX, 16, LAT), BF),
        pltpu.VMEM((NX, 16, LAT), F32),
        pltpu.VMEM((NX, 16, LAT), F32),
        pltpu.VMEM((16, LAT), F32),
        pltpu.VMEM((NY, 16, LAT), F32),
        pltpu.SemaphoreType.DMA((N_SEM,)),
        pltpu.SemaphoreType.DMA((N_SEM,)),
        pltpu.SemaphoreType.DMA((9,)),
    ]
    out, q_grad, lat_grad = pl.pallas_call(
        body,
        out_shape=(
            jax.ShapeDtypeStruct((TOK, WID), BF),
            jax.ShapeDtypeStruct((HEADS, TOK, LAT), BF),
            jax.ShapeDtypeStruct((4, LAT), F32),
        ),
        in_specs=[anywhere] * 8 + [vmem] + [anywhere],
        out_specs=(vmem, vmem, vmem),
        scratch_shapes=scratch,
        compiler_params=pltpu.CompilerParams(
            collective_id=0, has_side_effects=True, vmem_limit_bytes=63 * 2**20
        ),
    )(
        moe_input, moe_grad, meta, w_gate, w_up, w_down, q_heads, g_heads,
        positions.reshape(TOK, 1), latents,
    )
    return (out, q_grad.transpose(1, 0, 2).reshape(TOK, HEADS * LAT), lat_grad)


def solution(mesh):
    return jax.shard_map(
        per_device,
        mesh=mesh,
        in_specs=(
            P("exp", "ctx"),
            P("exp", "ctx"),
            P("exp", None),
            P("exp", None),
            P("exp", "ctx", None),
            P("exp", "ctx", None),
            P("exp", None, "ctx"),
            P("ctx", "exp"),
            P("ctx", "exp"),
            P("ctx"),
            P("ctx", None),
        ),
        out_specs=(P("exp", "ctx"), P("ctx", "exp"), P(("ctx", "exp"), None)),
        check_vma=False,
    )
```

```python
import jax
import jax.numpy as jnp
from jax import lax
from jax.experimental import pallas as pl
from jax.experimental.pallas import tpu as pltpu
from jax.sharding import PartitionSpec as P

SCORE_SCALE = 192.0 ** (-0.5)
MASKED = -1e30
MESH = pl.DeviceIdType.MESH
BF = jnp.bfloat16
F32 = jnp.float32

NX, NZ, NY, NC = 4, 8, 4, 2
NQ = NY * NC
TOK = 128
WID = 896
HID = 1024
CAP = 10
SLOTS = NZ * CAP
LAT = 576
VAL = 512
HEADS = 2
KEY_DEV = 256
KEYS = NX * KEY_DEV

PIECES = 4
N_ZAG = 2 * 2 * 4 * PIECES
N_META = 8
N_LAT = 4
N_PLANE = 16
N_BACK = 16
N_RS = 48
N_AG = 24
N_ZRS = 2 * 4 * PIECES
N_LG = 1 + 8 + 4 + 4

OFF_ZAG = 0
OFF_META = OFF_ZAG + N_ZAG
OFF_LAT = OFF_META + N_META
OFF_PLANE = OFF_LAT + N_LAT
OFF_BACK = OFF_PLANE + N_PLANE
OFF_RS = OFF_BACK + N_BACK
OFF_AG = OFF_RS + N_RS
OFF_ZRS = OFF_AG + N_AG
OFF_LG = OFF_ZRS + N_ZRS
N_SEM = OFF_LG + N_LG


def nn(a, b):
    return lax.dot_general(a, b, (((1,), (0,)), ((), ())), preferred_element_type=F32)


def nt(a, b):
    return lax.dot_general(a, b, (((1,), (1,)), ((), ())), preferred_element_type=F32)


def tn(a, b):
    return lax.dot_general(a, b, (((0,), (0,)), ((), ())), preferred_element_type=F32)


def body(
    in_hbm, grad_hbm, routes_ref, gates_ref, wg_hbm, wu_hbm, wd_hbm, q_hbm, og_hbm, pos_ref, lat_hbm,
    out_ref, qg_ref, lg_ref,
    tok, meta, wg, wu, wd, qv, ogv, latraw, lat, rank_s, gate_s, pick, ysend, yrecv,
    part, rs_mid, rs_in, bk, rsend, rrecv, zsend_v, zrecv,
    lacc, lout, lc_in, lz_out, lz_in, lx_out, lx_in, ly_out, ly_in,
    ssem, rsem, lsem,
):
    x = lax.axis_index("ctx")
    e_id = lax.axis_index("exp")
    z = e_id // NQ
    q = e_id % NQ
    y = q // NC
    c = q % NC

    def dev(xx, zz, qq):
        return (xx, zz * NQ + qq)

    def zdev(d):
        return dev(x, (z + d + NZ) % NZ, q)

    def xdev(d):
        return dev((x + d + NX) % NX, z, q)

    def plane(dy, dc):
        return ((y + dy + NY) % NY) * NC + (c + dc) % NC

    sends = []

    def copy(src, dst, idx, to):
        return pltpu.make_async_remote_copy(
            src_ref=src, dst_ref=dst, send_sem=ssem.at[idx], recv_sem=rsem.at[idx],
            device_id=to, device_id_type=MESH,
        )

    def send(src, dst, idx, to):
        op = copy(src, dst, idx, to)
        op.start()
        sends.append(op)

    def arrived(dst, idx, frm):
        copy(dst, dst, idx, frm).wait_recv()

    loads = []

    def load(src, dst):
        op = pltpu.make_async_copy(src, dst, lsem.at[len(loads)])
        op.start()
        loads.append(op)
        return op

    ld_in = load(in_hbm, tok.at[0, z])
    ld_lat = load(lat_hbm, latraw)
    ld_grad = load(grad_hbm, tok.at[1, z])
    ld_q = load(q_hbm, qv)
    ld_og = load(og_hbm, ogv)
    ld_wg = load(wg_hbm, wg)
    ld_wu = load(wu_hbm, wu)
    ld_wd = load(wd_hbm, wd)

    barrier = pltpu.get_barrier_semaphore()
    peers = [zdev(d) for d in range(1, NZ)]
    peers += [dev(x, z, plane(j // NC, j % NC)) for j in range(1, NQ)]
    peers += [xdev(d) for d in range(1, NX)]
    for peer in peers:
        pl.semaphore_signal(barrier, inc=1, device_id=peer, device_id_type=MESH)
    pl.semaphore_wait(barrier, len(peers))

    PR = TOK // PIECES

    def zidx(a, way, step, piece):
        return OFF_ZAG + ((a * 2 + way) * 4 + step) * PIECES + piece

    def pieces(way, step):
        if step < 3:
            return tuple(range(PIECES))
        return tuple(range(PIECES // 2)) if way == 0 else tuple(range(PIECES // 2, PIECES))

    def zpiece(a, way, dist, piece):
        b = (z - dist + NZ) % NZ if way == 0 else (z + dist) % NZ
        return tok.at[a, b, pl.ds(piece * PR, PR)]

    def zsend_piece(a, way, step, piece):
        blk = zpiece(a, way, step, piece)
        send(blk, blk, zidx(a, way, step, piece), zdev(1 if way == 0 else -1))

    def zsend(a):
        for piece in range(PIECES):
            for way in (0, 1):
                zsend_piece(a, way, 0, piece)

    def zforward(a, step):
        for piece in range(PIECES):
            for way in (0, 1):
                arrived(zpiece(a, way, step, piece), zidx(a, way, step - 1, piece), zdev(-1 if way == 0 else 1))
                if piece in pieces(way, step):
                    zsend_piece(a, way, step, piece)

    def zlast(a):
        for way in (0, 1):
            for piece in pieces(way, 3):
                arrived(zpiece(a, way, 4, piece), zidx(a, way, 3, piece), zdev(-1 if way == 0 else 1))

    ld_in.wait()
    zsend(0)
    meta[z, 0:8] = routes_ref[...].astype(F32)
    meta[z, 8:16] = gates_ref[...]
    for d in range(1, NZ):
        send(meta.at[z], meta.at[z], OFF_META + d, zdev(d))

    ld_lat.wait()
    new = lax.broadcasted_iota(jnp.int32, (KEY_DEV, KEY_DEV), 0)
    old = lax.broadcasted_iota(jnp.int32, (KEY_DEV, KEY_DEV), 1)
    src = ((new // 16) % 8) * 32 + ((new // 4) % 4) * 8 + (new // 128) * 4 + new % 4
    shuffle = jnp.where(src == old, 1.0, 0.0).astype(BF)
    lat[x] = nt(shuffle, latraw[...]).astype(BF)
    for d in range(1, NX):
        send(lat.at[x], lat.at[x], OFF_LAT + d, xdev(d))

    zforward(0, 1)

    for d in range(1, NZ):
        b = (z - d + NZ) % NZ
        arrived(meta.at[b], OFF_META + d, dev(x, b, q))
    tri = jnp.where(
        lax.broadcasted_iota(jnp.int32, (TOK, TOK), 0) < lax.broadcasted_iota(jnp.int32, (TOK, TOK), 1),
        1.0, 0.0,
    ).astype(BF)
    names = (lax.broadcasted_iota(jnp.int32, (2 * NQ, TOK), 0) + z * (2 * NQ)).astype(F32)
    for b in range(NZ):
        member = jnp.zeros((2 * NQ, TOK), F32)
        gate = jnp.zeros((2 * NQ, TOK), F32)
        for k in range(8):
            hit = meta[b, k : k + 1, :] == names
            member = jnp.where(hit, 1.0, member)
            gate = jnp.where(hit, meta[b, 8 + k : 9 + k, :], gate)
        rank = nn(member.astype(BF), tri)
        rank_s[b] = jnp.where(member > 0.0, rank, -1.0)
        gate_s[b] = gate

    def slot_value(b):
        row = lax.broadcasted_iota(jnp.int32, (SLOTS, TOK), 0)
        return jnp.where(row % NZ == b, row // NZ, -5).astype(F32)

    def build(weighted):
        for b in range(NZ):
            value = slot_value(b)

            def one(i, carry):
                row = rank_s[b, pl.ds(i, 1), :]
                if weighted:
                    cell = jnp.where(row == value, gate_s[b, pl.ds(i, 1), :], 0.0)
                else:
                    cell = jnp.where(row == value, 1.0, 0.0)
                pick[i, :, b * TOK : (b + 1) * TOK] = cell.astype(BF)
                return carry

            lax.fori_loop(0, 2 * NQ, one, 0)

    zforward(0, 2)
    build(False)
    zforward(0, 3)
    ld_grad.wait()
    zsend(1)

    ld_q.wait()
    ld_og.wait()
    for d in range(1, NX):
        arrived(lat.at[(x - d + NX) % NX], OFF_LAT + d, xdev(-d))

    col = lax.broadcasted_iota(jnp.int32, (TOK, KEYS), 1)
    key_pos = (
        (col // 256) * 256 + ((col // 16) % 8) * 32 + ((col // 4) % 4) * 8 + ((col // 128) % 2) * 4 + col % 4
    )

    eye = lax.broadcasted_iota(jnp.int32, (TOK, TOK), 0) == lax.broadcasted_iota(jnp.int32, (TOK, TOK), 1)
    row_pos = jnp.sum(jnp.where(eye, pos_ref[...].astype(F32), 0.0), axis=1, keepdims=True).astype(jnp.int32)

    def attention(h):
        keys = lat[...].reshape(KEYS, LAT)
        visible = key_pos <= row_pos
        qh = qv[:, h * LAT : (h + 1) * LAT]
        gh = ogv[:, h * VAL : (h + 1) * VAL]
        score = jnp.where(visible, nt(qh, keys) * SCORE_SCALE, MASKED)
        peak = jnp.max(score, axis=1, keepdims=True)
        raw = jnp.where(visible, jnp.exp(score - peak), 0.0)
        attend = raw / jnp.sum(raw, axis=1, keepdims=True)
        dots = nt(gh, keys[:, :VAL])
        row_dot = jnp.sum(attend * dots, axis=1, keepdims=True)
        grad = (attend * (dots - row_dot)).astype(BF)
        low = attend.astype(BF)
        qg_ref[:, h * LAT : (h + 1) * LAT] = (nn(grad, keys) * SCORE_SCALE).astype(BF)
        key_part = tn(grad, qh) * SCORE_SCALE
        val_part = tn(low, gh)
        if h == 0:
            lacc[...] = key_part
        else:
            lacc[...] += key_part
        lacc[:, :VAL] += val_part

    attention(0)
    zlast(0)

    def pidx(a, j):
        return OFF_PLANE + a * NQ + j

    both = pl.ds(0, 2)

    def pack(a, offsets):
        for j in offsets:
            qq = plane(j // NC, j % NC)
            toks = tok[a].reshape(NZ * TOK, WID)
            rows = nn(pick[pl.ds(qq * 2, 2)].reshape(2 * SLOTS, NZ * TOK), toks).astype(BF)
            rows = rows.reshape(2, SLOTS, WID)
            if j == 0:
                yrecv[a, :, q] = rows
            else:
                ysend[a, qq] = rows
                send(ysend.at[a, qq], yrecv.at[a, both, q], pidx(a, j), dev(x, z, qq))

    def rows_arrive(a, s):
        for dc in range(NC):
            j = s * NC + dc
            if j:
                frm = plane(-s, dc)
                arrived(yrecv.at[a, both, frm], pidx(a, j), dev(x, z, frm))

    k_opp, k_right, k_left = (x + 2) % NX, (x + 1) % NX, (x + 3) % NX
    right, left = xdev(1), xdev(-1)
    low, high = pl.ds(0, HID // 2), pl.ds(HID // 2, HID // 2)
    every = pl.ds(0, SLOTS)
    UNITS = ((0, 2, ("gate", "up")), (2, 1, ("down",)))

    def partial(s, name, k):
        a, w = {"gate": (0, wg), "up": (0, wu), "down": (1, wd)}[name]
        e = k // NC
        rows = yrecv[a, e, plane(-s, 0) // NC * NC + k % NC]
        return nt(rows, w[e]) if name == "down" else nn(rows, w[e])

    def ridx(s, u, n):
        return OFF_RS + (s * 2 + u) * 6 + n

    def store_part(s, u, k):
        first, _, names_ = UNITS[u]
        for i, name in enumerate(names_):
            part[s, k, first + i] = partial(s, name, k).astype(BF)

    def reduce_first(s, u):
        first, n, _ = UNITS[u]
        rng = pl.ds(first, n)
        store_part(s, u, k_opp)
        send(part.at[s, k_opp, rng, every, low], rs_mid.at[0, s, rng], ridx(s, u, 0), right)
        send(part.at[s, k_opp, rng, every, high], rs_mid.at[1, s, rng], ridx(s, u, 1), left)
        store_part(s, u, k_right)
        send(part.at[s, k_right, rng, every, high], rs_in.at[0, s, rng, every, high], ridx(s, u, 2), right)
        store_part(s, u, k_left)
        send(part.at[s, k_left, rng, every, low], rs_in.at[1, s, rng, every, low], ridx(s, u, 3), left)

    def reduce_second(s, u):
        first, n, _ = UNITS[u]
        rng = pl.ds(first, n)
        for way, frm, to, k, cols in ((0, left, right, k_right, low), (1, right, left, k_left, high)):
            arrived(rs_mid.at[way, s, rng], ridx(s, u, way), frm)
            got = rs_mid[way, s, rng].astype(F32) + part[s, k, rng, :, cols].astype(F32)
            part[s, k, rng, :, cols] = got.astype(BF)
            send(part.at[s, k, rng, every, cols], rs_in.at[way, s, rng, every, cols], ridx(s, u, 4 + way), to)
        store_part(s, u, x)

    def reduce_last(s):
        for u in (0, 1):
            first, n, _ = UNITS[u]
            rng = pl.ds(first, n)
            arrived(rs_in.at[0, s, rng, every, high], ridx(s, u, 2), left)
            arrived(rs_in.at[1, s, rng, every, low], ridx(s, u, 3), right)
            arrived(rs_in.at[0, s, rng, every, low], ridx(s, u, 4), left)
            arrived(rs_in.at[1, s, rng, every, high], ridx(s, u, 5), right)

    def total(s, i):
        return part[s, x, i].astype(F32) + rs_in[0, s, i].astype(F32) + rs_in[1, s, i].astype(F32)

    def aidx(s, way, n):
        return OFF_AG + (s * 2 + way) * 3 + n

    def bk_cols(s, k, cols):
        return bk.at[s, k, both, every, cols]

    def swiglu_back(s):
        gate_pre, up_pre, hidden = (total(s, i) for i in range(3))
        sigma = jax.nn.sigmoid(gate_pre)
        bk[s, x, 0] = (hidden * up_pre * sigma * (1.0 + gate_pre * (1.0 - sigma))).astype(BF)
        bk[s, x, 1] = (hidden * gate_pre * sigma).astype(BF)
        t, b = bk_cols(s, x, low), bk_cols(s, x, high)
        send(t, t, aidx(s, 0, 0), right)
        send(b, b, aidx(s, 1, 0), left)
        send(b, b, aidx(s, 0, 1), right)
        send(t, t, aidx(s, 1, 1), left)

    def gather_forward(s):
        t, b = bk_cols(s, k_left, low), bk_cols(s, k_right, high)
        arrived(t, aidx(s, 0, 0), left)
        send(t, t, aidx(s, 0, 2), right)
        arrived(b, aidx(s, 1, 0), right)
        send(b, b, aidx(s, 1, 2), left)

    def gather_near(s):
        arrived(bk_cols(s, k_left, high), aidx(s, 0, 1), left)
        arrived(bk_cols(s, k_right, low), aidx(s, 1, 1), right)

    def gather_far(s):
        arrived(bk_cols(s, k_opp, low), aidx(s, 0, 2), left)
        arrived(bk_cols(s, k_opp, high), aidx(s, 1, 2), right)

    def bidx(s, e, dc):
        return OFF_BACK + (s * 2 + e) * NC + dc

    def route(s, k):
        e, cs = k // NC, k % NC
        dc = (cs + c) % NC
        qq = plane(-s, 0) // NC * NC + cs
        rows = (nt(bk[s, k, 0], wg[e]) + nt(bk[s, k, 1], wu[e])).astype(BF)
        if s:
            rsend[s, k] = rows
            copy(rsend.at[s, k], rrecv.at[q, e], bidx(s, e, dc), dev(x, z, qq)).start()
        else:

            @pl.when(dc != 0)
            def _():
                rsend[s, k] = rows
                copy(rsend.at[s, k], rrecv.at[q, e], bidx(s, e, 1), dev(x, z, plane(0, 1))).start()

            @pl.when(dc == 0)
            def _():
                rrecv[q, e] = rows

    def route_near(s):
        route(s, x)
        gather_near(s)
        route(s, k_left)
        route(s, k_right)

    def route_far(s):
        gather_far(s)
        route(s, k_opp)

    sib = plane(0, 1)

    def latent_start():
        lout[...] = lacc[...].astype(BF).reshape(NX, NC, 128, LAT)
        send(lout.at[:, 1 - c], lc_in, OFF_LG, dev(x, z, sib))

    def latent_z():
        arrived(lc_in, OFF_LG, dev(x, z, sib))
        mine = lacc[...].reshape(NX, NC, 128, LAT)
        summed = jnp.where(c == 0, mine[:, 0], mine[:, 1]) + lc_in[...].astype(F32)
        lacc[pl.ds(0, NX * 128)] = summed.reshape(NX * 128, LAT)
        lz_out[...] = summed.astype(BF).reshape(NX, NZ, 16, LAT)
        for d in range(1, NZ):
            send(lz_out.at[:, (z + d) % NZ], lz_in.at[d], OFF_LG + d, zdev(d))

    def latent_x():
        zsum = lacc[pl.ds(0, NX * 128)].reshape(NX, NZ, 16, LAT)
        zown = jnp.where(z == 0, zsum[:, 0], 0.0)
        for b in range(1, NZ):
            zown = zown + jnp.where(z == b, zsum[:, b], 0.0)
        for d in range(1, NZ):
            arrived(lz_in.at[d], OFF_LG + d, zdev(-d))
            zown = zown + lz_in[d].astype(F32)
        lx_out[...] = zown
        for d in range(1, NX):
            send(lx_out.at[(x + d) % NX], lx_in.at[d], OFF_LG + 8 + d, xdev(d))

    def latent_y():
        xsum = lx_out[x]
        for d in range(1, NX):
            arrived(lx_in.at[d], OFF_LG + 8 + d, xdev(-d))
            xsum = xsum + lx_in[d]
        ly_out[...] = xsum
        for d in range(1, NY):
            send(ly_out, ly_in.at[d], OFF_LG + 12 + d, dev(x, z, plane(d, 0)))

    def latent_end():
        ysum = ly_out[...]
        for d in range(1, NY):
            arrived(ly_in.at[d], OFF_LG + 12 + d, dev(x, z, plane(-d, 0)))
            ysum = ysum + ly_in[d]
        pick4 = jnp.where(y == 0, ysum[0:4], 0.0)
        for b in range(1, NY):
            pick4 = pick4 + jnp.where(y == b, ysum[4 * b : 4 * b + 4], 0.0)
        lg_ref[...] = pick4

    pack(0, (1, 0, 2, 3, 6, 7))
    ld_wg.wait()
    ld_wu.wait()
    ld_wd.wait()
    rows_arrive(0, 0)
    reduce_first(0, 0)
    pack(0, (4, 5))
    zforward(1, 1)
    attention(1)
    latent_start()
    rows_arrive(0, 1)
    reduce_first(1, 0)
    reduce_second(0, 0)
    zforward(1, 2)
    rows_arrive(0, 3)
    reduce_first(3, 0)
    reduce_second(1, 0)
    latent_z()
    zforward(1, 3)
    rows_arrive(0, 2)
    reduce_first(2, 0)
    reduce_second(3, 0)
    zlast(1)
    pack(1, (4, 5, 2, 3, 6, 7, 1, 0))
    build(True)
    rows_arrive(1, 2)
    reduce_first(2, 1)
    reduce_second(2, 0)
    latent_x()
    rows_arrive(1, 1)
    reduce_first(1, 1)
    reduce_second(2, 1)
    rows_arrive(1, 3)
    reduce_first(3, 1)
    reduce_second(1, 1)
    reduce_last(2)
    swiglu_back(2)
    rows_arrive(1, 0)
    reduce_first(0, 1)
    reduce_second(3, 1)
    latent_y()
    reduce_last(1)
    swiglu_back(1)
    gather_forward(2)
    reduce_second(0, 1)
    reduce_last(3)
    swiglu_back(3)
    route_near(2)
    gather_forward(1)
    reduce_last(0)
    swiglu_back(0)
    route_far(2)
    gather_forward(3)
    route_near(1)
    route_far(1)
    gather_forward(0)
    latent_end()
    route_near(3)
    route_far(3)
    route_near(0)
    route_far(0)

    for s in (2, 1, 3, 0):
        for e in (0, 1):
            for dc in range(NC):
                if s or dc:
                    frm = plane(s, dc)
                    arrived(rrecv.at[frm, e], bidx(s, e, dc), dev(x, z, frm))

    def tokens(b):
        cols = pl.ds(pl.multiple_of(b * TOK, TOK), TOK)
        return tn(
            pick[:, :, cols].reshape(2 * NQ * SLOTS, TOK), rrecv[...].reshape(2 * NQ * SLOTS, WID)
        )

    def widx(way, step, piece):
        return OFF_ZRS + (way * 4 + step) * PIECES + piece

    def zsum_send(way, step, piece):
        rows = pl.ds(piece * PR, PR)
        to = zdev(1 if way == 0 else -1)
        send(zsend_v.at[way, step, rows], zrecv.at[way, step, rows], widx(way, step, piece), to)

    def zsum_got(way, step, piece):
        rows = pl.ds(piece * PR, PR)
        arrived(zrecv.at[way, step, rows], widx(way, step, piece), zdev(-1 if way == 0 else 1))
        return zrecv[way, step, rows].astype(F32)

    far = tokens((z + 4) % NZ).astype(BF)
    for way in (0, 1):
        for piece in pieces(way, 3):
            zsend_v[way, 0, pl.ds(piece * PR, PR)] = far[piece * PR : (piece + 1) * PR]
            zsum_send(way, 0, piece)
    for step in (1, 2, 3):
        accs = [tokens((z + 4 - step) % NZ), tokens((z + 4 + step) % NZ)]
        for piece in range(PIECES):
            for way in (0, 1):
                rows = accs[way][piece * PR : (piece + 1) * PR]
                if step > 1 or piece in pieces(way, 3):
                    rows = rows + zsum_got(way, step - 1, piece)
                zsend_v[way, step, pl.ds(piece * PR, PR)] = rows.astype(BF)
                zsum_send(way, step, piece)
    final = tokens(z)
    for piece in range(PIECES):
        rows = final[piece * PR : (piece + 1) * PR]
        for way in (0, 1):
            rows = rows + zsum_got(way, 3, piece)
        out_ref[pl.ds(piece * PR, PR)] = rows.astype(BF)

    for op in sends:
        op.wait_send()
    for s in range(NY):
        for e in (0, 1):
            for dc in range(NC):
                if s or dc:
                    copy(rsend.at[s, 0], rrecv.at[0, e], bidx(s, e, dc), dev(x, z, plane(-s, dc))).wait_send()


def settle(a_ref, b_ref, c_ref, x_ref, y_ref, z_ref):
    x_ref[...] = a_ref[...]
    y_ref[...] = b_ref[...]
    z_ref[...] = c_ref[...]


def per_device(
    moe_input, moe_grad, routes, gates, w_gate, w_up, w_down, queries, out_grad, positions, latents
):
    anywhere = pl.BlockSpec(memory_space=pl.ANY)
    vmem = pl.BlockSpec(memory_space=pltpu.VMEM)
    scratch = [
        pltpu.VMEM((2, NZ, TOK, WID), BF),
        pltpu.VMEM((NZ, 16, TOK), F32),
        pltpu.VMEM((2, WID, HID), BF),
        pltpu.VMEM((2, WID, HID), BF),
        pltpu.VMEM((2, HID, WID), BF),
        pltpu.VMEM((TOK, HEADS * LAT), BF),
        pltpu.VMEM((TOK, HEADS * VAL), BF),
        pltpu.VMEM((LAT, KEY_DEV), BF),
        pltpu.VMEM((NX, KEY_DEV, LAT), BF),
        pltpu.VMEM((NZ, 2 * NQ, TOK), F32),
        pltpu.VMEM((NZ, 2 * NQ, TOK), F32),
        pltpu.VMEM((2 * NQ, SLOTS, NZ * TOK), BF),
        pltpu.VMEM((2, NQ, 2, SLOTS, WID), BF),
        pltpu.VMEM((2, 2, NQ, SLOTS, WID), BF),
        pltpu.VMEM((NY, NX, 3, SLOTS, HID), BF),
        pltpu.VMEM((2, NY, 3, SLOTS, HID // 2), BF),
        pltpu.VMEM((2, NY, 3, SLOTS, HID), BF),
        pltpu.VMEM((NY, NX, 2, SLOTS, HID), BF),
        pltpu.VMEM((NY, NX, SLOTS, WID), BF),
        pltpu.VMEM((NQ, 2, SLOTS, WID), BF),
        pltpu.VMEM((2, 4, TOK, WID), BF),
        pltpu.VMEM((2, 4, TOK, WID), BF),
        pltpu.VMEM((KEYS, LAT), F32),
        pltpu.VMEM((NX, NC, 128, LAT), BF),
        pltpu.VMEM((NX, 128, LAT), BF),
        pltpu.VMEM((NX, NZ, 16, LAT), BF),
        pltpu.VMEM((NZ, NX, 16, LAT), BF),
        pltpu.VMEM((NX, 16, LAT), F32),
        pltpu.VMEM((NX, 16, LAT), F32),
        pltpu.VMEM((16, LAT), F32),
        pltpu.VMEM((NY, 16, LAT), F32),
        pltpu.SemaphoreType.DMA((N_SEM,)),
        pltpu.SemaphoreType.DMA((N_SEM,)),
        pltpu.SemaphoreType.DMA((9,)),
    ]
    out, q_grad, lat_grad = pl.pallas_call(
        body,
        out_shape=(
            jax.ShapeDtypeStruct((TOK, WID), BF),
            jax.ShapeDtypeStruct((TOK, HEADS * LAT), BF),
            jax.ShapeDtypeStruct((4, LAT), F32),
        ),
        in_specs=[anywhere] * 2 + [vmem] * 2 + [anywhere] * 5 + [vmem] + [anywhere],
        out_specs=(vmem, vmem, vmem),
        scratch_shapes=scratch,
        compiler_params=pltpu.CompilerParams(
            collective_id=0, has_side_effects=True, vmem_limit_bytes=63 * 2**20
        ),
    )(
        moe_input, moe_grad, routes.T, gates.T, w_gate, w_up, w_down, queries, out_grad,
        positions.reshape(1, TOK), latents.T,
    )
    return pl.pallas_call(
        settle,
        out_shape=[jax.ShapeDtypeStruct(v.shape, v.dtype) for v in (out, q_grad, lat_grad)],
        in_specs=[vmem] * 3,
        out_specs=[vmem] * 3,
    )(out, q_grad, lat_grad)


def solution(mesh):
    return jax.shard_map(
        per_device,
        mesh=mesh,
        in_specs=(
            P("exp", "ctx"),
            P("exp", "ctx"),
            P("exp", None),
            P("exp", None),
            P("exp", "ctx", None),
            P("exp", "ctx", None),
            P("exp", None, "ctx"),
            P("ctx", "exp"),
            P("ctx", "exp"),
            P("ctx"),
            P("ctx", None),
        ),
        out_specs=(P("exp", "ctx"), P("ctx", "exp"), P(("ctx", "exp"), None)),
        check_vma=False,
    )
```

```python
import jax
import jax.numpy as jnp
from jax import lax
from jax.experimental import pallas as pl
from jax.experimental.pallas import tpu as pltpu
from jax.sharding import PartitionSpec as P

SCORE_SCALE = 192.0 ** (-0.5)
MASKED = -1e30
MESH = pl.DeviceIdType.MESH
BF = jnp.bfloat16
F32 = jnp.float32

NX, NZ, NY, NC = 4, 8, 4, 2
NQ = NY * NC
TOK = 128
WID = 896
HID = 1024
CAP = 10
SLOTS = NZ * CAP
LAT = 576
VAL = 512
HEADS = 2
KEY_DEV = 256
KEYS = NX * KEY_DEV

PIECES = 4
N_ZAG = 2 * 2 * 4 * PIECES
N_META = 8
N_LAT = 4
N_PLANE = 16
N_BACK = 16
N_RS = 48
N_AG = 24
N_ZRS = 2 * 4 * PIECES
N_LG = 1 + 8 + 4 + 4

OFF_ZAG = 0
OFF_META = OFF_ZAG + N_ZAG
OFF_LAT = OFF_META + N_META
OFF_PLANE = OFF_LAT + N_LAT
OFF_BACK = OFF_PLANE + N_PLANE
OFF_RS = OFF_BACK + N_BACK
OFF_AG = OFF_RS + N_RS
OFF_ZRS = OFF_AG + N_AG
OFF_LG = OFF_ZRS + N_ZRS
N_SEM = OFF_LG + N_LG


def nn(a, b):
    return lax.dot_general(a, b, (((1,), (0,)), ((), ())), preferred_element_type=F32)


def nt(a, b):
    return lax.dot_general(a, b, (((1,), (1,)), ((), ())), preferred_element_type=F32)


def tn(a, b):
    return lax.dot_general(a, b, (((0,), (0,)), ((), ())), preferred_element_type=F32)


def body(
    in_hbm, grad_hbm, routes_ref, gates_ref, wg_hbm, wu_hbm, wd_hbm, q_hbm, og_hbm, pos_ref, lat_hbm,
    out_ref, qg_ref, lg_ref,
    tok, meta, wg, wu, wd, qv, ogv, latraw, lat, rank_s, gate_s, pick, ysend, yrecv,
    part, rs_mid, rs_in, bk, rsend, rrecv, zsend_v, zrecv,
    lacc, lout, lc_in, lz_out, lz_in, lx_out, lx_in, ly_out, ly_in,
    ssem, rsem, lsem,
):
    x = lax.axis_index("ctx")
    e_id = lax.axis_index("exp")
    z = e_id // NQ
    q = e_id % NQ
    y = q // NC
    c = q % NC

    def dev(xx, zz, qq):
        return (xx, zz * NQ + qq)

    def zdev(d):
        return dev(x, (z + d + NZ) % NZ, q)

    def xdev(d):
        return dev((x + d + NX) % NX, z, q)

    def plane(dy, dc):
        return ((y + dy + NY) % NY) * NC + (c + dc) % NC

    sends = []

    def copy(src, dst, idx, to):
        return pltpu.make_async_remote_copy(
            src_ref=src, dst_ref=dst, send_sem=ssem.at[idx], recv_sem=rsem.at[idx],
            device_id=to, device_id_type=MESH,
        )

    def send(src, dst, idx, to):
        op = copy(src, dst, idx, to)
        op.start()
        sends.append(op)

    def arrived(dst, idx, frm):
        copy(dst, dst, idx, frm).wait_recv()

    loads = []

    def load(src, dst):
        op = pltpu.make_async_copy(src, dst, lsem.at[len(loads)])
        op.start()
        loads.append(op)
        return op

    ld_in = load(in_hbm, tok.at[0, z])
    ld_lat = load(lat_hbm, latraw)
    ld_grad = load(grad_hbm, tok.at[1, z])
    ld_q = load(q_hbm, qv)
    ld_og = load(og_hbm, ogv)
    ld_wg = load(wg_hbm, wg)
    ld_wu = load(wu_hbm, wu)
    ld_wd = load(wd_hbm, wd)

    barrier = pltpu.get_barrier_semaphore()
    peers = [zdev(d) for d in range(1, NZ)]
    peers += [dev(x, z, plane(j // NC, j % NC)) for j in range(1, NQ)]
    peers += [xdev(d) for d in range(1, NX)]
    for peer in peers:
        pl.semaphore_signal(barrier, inc=1, device_id=peer, device_id_type=MESH)
    pl.semaphore_wait(barrier, len(peers))

    PR = TOK // PIECES

    def zidx(a, way, step, piece):
        return OFF_ZAG + ((a * 2 + way) * 4 + step) * PIECES + piece

    def pieces(way, step):
        if step < 3:
            return tuple(range(PIECES))
        return tuple(range(PIECES // 2)) if way == 0 else tuple(range(PIECES // 2, PIECES))

    def zpiece(a, way, dist, piece):
        b = (z - dist + NZ) % NZ if way == 0 else (z + dist) % NZ
        return tok.at[a, b, pl.ds(piece * PR, PR)]

    def zsend_piece(a, way, step, piece):
        blk = zpiece(a, way, step, piece)
        send(blk, blk, zidx(a, way, step, piece), zdev(1 if way == 0 else -1))

    def zsend(a):
        for piece in range(PIECES):
            for way in (0, 1):
                zsend_piece(a, way, 0, piece)

    def zforward(a, step):
        for piece in range(PIECES):
            for way in (0, 1):
                arrived(zpiece(a, way, step, piece), zidx(a, way, step - 1, piece), zdev(-1 if way == 0 else 1))
                if piece in pieces(way, step):
                    zsend_piece(a, way, step, piece)

    def zlast(a):
        for way in (0, 1):
            for piece in pieces(way, 3):
                arrived(zpiece(a, way, 4, piece), zidx(a, way, 3, piece), zdev(-1 if way == 0 else 1))

    ld_in.wait()
    zsend(0)
    meta[z, 0:8] = routes_ref[...].astype(F32)
    meta[z, 8:16] = gates_ref[...]
    for d in range(1, NZ):
        send(meta.at[z], meta.at[z], OFF_META + d, zdev(d))

    ld_lat.wait()
    new = lax.broadcasted_iota(jnp.int32, (KEY_DEV, KEY_DEV), 0)
    old = lax.broadcasted_iota(jnp.int32, (KEY_DEV, KEY_DEV), 1)
    src = ((new // 16) % 8) * 32 + ((new // 4) % 4) * 8 + (new // 128) * 4 + new % 4
    shuffle = jnp.where(src == old, 1.0, 0.0).astype(BF)
    lat[x] = nt(shuffle, latraw[...]).astype(BF)
    for d in range(1, NX):
        send(lat.at[x], lat.at[x], OFF_LAT + d, xdev(d))

    zforward(0, 1)

    for d in range(1, NZ):
        b = (z - d + NZ) % NZ
        arrived(meta.at[b], OFF_META + d, dev(x, b, q))
    tri = jnp.where(
        lax.broadcasted_iota(jnp.int32, (TOK, TOK), 0) < lax.broadcasted_iota(jnp.int32, (TOK, TOK), 1),
        1.0, 0.0,
    ).astype(BF)
    names = (lax.broadcasted_iota(jnp.int32, (2 * NQ, TOK), 0) + z * (2 * NQ)).astype(F32)
    for b in range(NZ):
        member = jnp.zeros((2 * NQ, TOK), F32)
        gate = jnp.zeros((2 * NQ, TOK), F32)
        for k in range(8):
            hit = meta[b, k : k + 1, :] == names
            member = jnp.where(hit, 1.0, member)
            gate = jnp.where(hit, meta[b, 8 + k : 9 + k, :], gate)
        rank = nn(member.astype(BF), tri)
        rank_s[b] = jnp.where(member > 0.0, rank, -1.0)
        gate_s[b] = gate

    def slot_value(b):
        row = lax.broadcasted_iota(jnp.int32, (SLOTS, TOK), 0)
        return jnp.where(row % NZ == b, row // NZ, -5).astype(F32)

    def build(weighted):
        for b in range(NZ):
            value = slot_value(b)

            def one(i, carry):
                row = rank_s[b, pl.ds(i, 1), :]
                if weighted:
                    cell = jnp.where(row == value, gate_s[b, pl.ds(i, 1), :], 0.0)
                else:
                    cell = jnp.where(row == value, 1.0, 0.0)
                pick[i, :, b * TOK : (b + 1) * TOK] = cell.astype(BF)
                return carry

            lax.fori_loop(0, 2 * NQ, one, 0)

    zforward(0, 2)
    build(False)
    zforward(0, 3)
    ld_grad.wait()
    zsend(1)

    col = lax.broadcasted_iota(jnp.int32, (TOK, KEYS), 1)
    key_pos = (
        (col // 256) * 256 + ((col // 16) % 8) * 32 + ((col // 4) % 4) * 8 + ((col // 128) % 2) * 4 + col % 4
    )

    eye = lax.broadcasted_iota(jnp.int32, (TOK, TOK), 0) == lax.broadcasted_iota(jnp.int32, (TOK, TOK), 1)
    row_pos = jnp.sum(jnp.where(eye, pos_ref[...].astype(F32), 0.0), axis=1, keepdims=True).astype(jnp.int32)

    def attention(h):
        keys = lat[...].reshape(KEYS, LAT)
        visible = key_pos <= row_pos
        qh = qv[:, h * LAT : (h + 1) * LAT]
        gh = ogv[:, h * VAL : (h + 1) * VAL]
        score = jnp.where(visible, nt(qh, keys) * SCORE_SCALE, MASKED)
        peak = jnp.max(score, axis=1, keepdims=True)
        raw = jnp.where(visible, jnp.exp(score - peak), 0.0)
        attend = raw / jnp.sum(raw, axis=1, keepdims=True)
        dots = nt(gh, keys[:, :VAL])
        row_dot = jnp.sum(attend * dots, axis=1, keepdims=True)
        grad = (attend * (dots - row_dot)).astype(BF)
        low = attend.astype(BF)
        qg_ref[:, h * LAT : (h + 1) * LAT] = (nn(grad, keys) * SCORE_SCALE).astype(BF)
        key_part = tn(grad, qh) * SCORE_SCALE
        val_part = tn(low, gh)
        if h == 0:
            lacc[...] = key_part
        else:
            lacc[...] += key_part
        lacc[:, :VAL] += val_part

    zlast(0)

    def pidx(a, j):
        return OFF_PLANE + a * NQ + j

    both = pl.ds(0, 2)

    def pack(a, offsets):
        for j in offsets:
            qq = plane(j // NC, j % NC)
            toks = tok[a].reshape(NZ * TOK, WID)
            rows = nn(pick[pl.ds(qq * 2, 2)].reshape(2 * SLOTS, NZ * TOK), toks).astype(BF)
            rows = rows.reshape(2, SLOTS, WID)
            if j == 0:
                yrecv[a, :, q] = rows
            else:
                ysend[a, qq] = rows
                send(ysend.at[a, qq], yrecv.at[a, both, q], pidx(a, j), dev(x, z, qq))

    def rows_arrive(a, s):
        for dc in range(NC):
            j = s * NC + dc
            if j:
                frm = plane(-s, dc)
                arrived(yrecv.at[a, both, frm], pidx(a, j), dev(x, z, frm))

    k_opp, k_right, k_left = (x + 2) % NX, (x + 1) % NX, (x + 3) % NX
    right, left = xdev(1), xdev(-1)
    low, high = pl.ds(0, HID // 2), pl.ds(HID // 2, HID // 2)
    every = pl.ds(0, SLOTS)
    UNITS = ((0, 2, ("gate", "up")), (2, 1, ("down",)))

    def partial(s, name, k):
        a, w = {"gate": (0, wg), "up": (0, wu), "down": (1, wd)}[name]
        e = k // NC
        rows = yrecv[a, e, plane(-s, 0) // NC * NC + k % NC]
        return nt(rows, w[e]) if name == "down" else nn(rows, w[e])

    def ridx(s, u, n):
        return OFF_RS + (s * 2 + u) * 6 + n

    def store_part(s, u, k):
        first, _, names_ = UNITS[u]
        for i, name in enumerate(names_):
            part[s, k, first + i] = partial(s, name, k).astype(BF)

    def reduce_first(s, u):
        first, n, _ = UNITS[u]
        rng = pl.ds(first, n)
        store_part(s, u, k_opp)
        send(part.at[s, k_opp, rng, every, low], rs_mid.at[0, s, rng], ridx(s, u, 0), right)
        send(part.at[s, k_opp, rng, every, high], rs_mid.at[1, s, rng], ridx(s, u, 1), left)
        store_part(s, u, k_right)
        send(part.at[s, k_right, rng, every, high], rs_in.at[0, s, rng, every, high], ridx(s, u, 2), right)
        store_part(s, u, k_left)
        send(part.at[s, k_left, rng, every, low], rs_in.at[1, s, rng, every, low], ridx(s, u, 3), left)

    def reduce_second(s, u):
        first, n, _ = UNITS[u]
        rng = pl.ds(first, n)
        for way, frm, to, k, cols in ((0, left, right, k_right, low), (1, right, left, k_left, high)):
            arrived(rs_mid.at[way, s, rng], ridx(s, u, way), frm)
            got = rs_mid[way, s, rng].astype(F32) + part[s, k, rng, :, cols].astype(F32)
            part[s, k, rng, :, cols] = got.astype(BF)
            send(part.at[s, k, rng, every, cols], rs_in.at[way, s, rng, every, cols], ridx(s, u, 4 + way), to)
        store_part(s, u, x)

    def reduce_last(s):
        for u in (0, 1):
            first, n, _ = UNITS[u]
            rng = pl.ds(first, n)
            arrived(rs_in.at[0, s, rng, every, high], ridx(s, u, 2), left)
            arrived(rs_in.at[1, s, rng, every, low], ridx(s, u, 3), right)
            arrived(rs_in.at[0, s, rng, every, low], ridx(s, u, 4), left)
            arrived(rs_in.at[1, s, rng, every, high], ridx(s, u, 5), right)

    def total(s, i):
        return part[s, x, i].astype(F32) + rs_in[0, s, i].astype(F32) + rs_in[1, s, i].astype(F32)

    def aidx(s, way, n):
        return OFF_AG + (s * 2 + way) * 3 + n

    def bk_cols(s, k, cols):
        return bk.at[s, k, both, every, cols]

    def swiglu_back(s):
        gate_pre, up_pre, hidden = (total(s, i) for i in range(3))
        sigma = jax.nn.sigmoid(gate_pre)
        bk[s, x, 0] = (hidden * up_pre * sigma * (1.0 + gate_pre * (1.0 - sigma))).astype(BF)
        bk[s, x, 1] = (hidden * gate_pre * sigma).astype(BF)
        t, b = bk_cols(s, x, low), bk_cols(s, x, high)
        send(t, t, aidx(s, 0, 0), right)
        send(b, b, aidx(s, 1, 0), left)
        send(b, b, aidx(s, 0, 1), right)
        send(t, t, aidx(s, 1, 1), left)

    def gather_forward(s):
        t, b = bk_cols(s, k_left, low), bk_cols(s, k_right, high)
        arrived(t, aidx(s, 0, 0), left)
        send(t, t, aidx(s, 0, 2), right)
        arrived(b, aidx(s, 1, 0), right)
        send(b, b, aidx(s, 1, 2), left)

    def gather_near(s):
        arrived(bk_cols(s, k_left, high), aidx(s, 0, 1), left)
        arrived(bk_cols(s, k_right, low), aidx(s, 1, 1), right)

    def gather_far(s):
        arrived(bk_cols(s, k_opp, low), aidx(s, 0, 2), left)
        arrived(bk_cols(s, k_opp, high), aidx(s, 1, 2), right)

    def bidx(s, e, dc):
        return OFF_BACK + (s * 2 + e) * NC + dc

    def route(s, k):
        e, cs = k // NC, k % NC
        dc = (cs + c) % NC
        qq = plane(-s, 0) // NC * NC + cs
        rows = (nt(bk[s, k, 0], wg[e]) + nt(bk[s, k, 1], wu[e])).astype(BF)
        if s:
            rsend[s, k] = rows
            copy(rsend.at[s, k], rrecv.at[q, e], bidx(s, e, dc), dev(x, z, qq)).start()
        else:

            @pl.when(dc != 0)
            def _():
                rsend[s, k] = rows
                copy(rsend.at[s, k], rrecv.at[q, e], bidx(s, e, 1), dev(x, z, plane(0, 1))).start()

            @pl.when(dc == 0)
            def _():
                rrecv[q, e] = rows

    def route_near(s):
        route(s, x)
        gather_near(s)
        route(s, k_left)
        route(s, k_right)

    def route_far(s):
        gather_far(s)
        route(s, k_opp)

    sib = plane(0, 1)

    def latent_start():
        lout[...] = lacc[...].astype(BF).reshape(NX, NC, 128, LAT)
        send(lout.at[:, 1 - c], lc_in, OFF_LG, dev(x, z, sib))

    def latent_z():
        arrived(lc_in, OFF_LG, dev(x, z, sib))
        mine = lacc[...].reshape(NX, NC, 128, LAT)
        summed = jnp.where(c == 0, mine[:, 0], mine[:, 1]) + lc_in[...].astype(F32)
        lacc[pl.ds(0, NX * 128)] = summed.reshape(NX * 128, LAT)
        lz_out[...] = summed.astype(BF).reshape(NX, NZ, 16, LAT)
        for d in range(1, NZ):
            send(lz_out.at[:, (z + d) % NZ], lz_in.at[d], OFF_LG + d, zdev(d))

    def latent_x():
        zsum = lacc[pl.ds(0, NX * 128)].reshape(NX, NZ, 16, LAT)
        zown = jnp.where(z == 0, zsum[:, 0], 0.0)
        for b in range(1, NZ):
            zown = zown + jnp.where(z == b, zsum[:, b], 0.0)
        for d in range(1, NZ):
            arrived(lz_in.at[d], OFF_LG + d, zdev(-d))
            zown = zown + lz_in[d].astype(F32)
        lx_out[...] = zown
        for d in range(1, NX):
            send(lx_out.at[(x + d) % NX], lx_in.at[d], OFF_LG + 8 + d, xdev(d))

    def latent_y():
        xsum = lx_out[x]
        for d in range(1, NX):
            arrived(lx_in.at[d], OFF_LG + 8 + d, xdev(-d))
            xsum = xsum + lx_in[d]
        ly_out[...] = xsum
        for d in range(1, NY):
            send(ly_out, ly_in.at[d], OFF_LG + 12 + d, dev(x, z, plane(d, 0)))

    def latent_end():
        ysum = ly_out[...]
        for d in range(1, NY):
            arrived(ly_in.at[d], OFF_LG + 12 + d, dev(x, z, plane(-d, 0)))
            ysum = ysum + ly_in[d]
        pick4 = jnp.where(y == 0, ysum[0:4], 0.0)
        for b in range(1, NY):
            pick4 = pick4 + jnp.where(y == b, ysum[4 * b : 4 * b + 4], 0.0)
        lg_ref[...] = pick4

    pack(0, (1, 0, 2, 3, 6, 7))
    ld_wg.wait()
    ld_wu.wait()
    ld_wd.wait()
    rows_arrive(0, 0)
    reduce_first(0, 0)
    pack(0, (4, 5))
    zforward(1, 1)
    ld_q.wait()
    ld_og.wait()
    for d in range(1, NX):
        arrived(lat.at[(x - d + NX) % NX], OFF_LAT + d, xdev(-d))
    attention(0)
    zforward(1, 2)
    reduce_second(0, 0)
    rows_arrive(0, 1)
    reduce_first(1, 0)
    rows_arrive(0, 3)
    reduce_first(3, 0)
    zforward(1, 3)
    reduce_second(1, 0)
    attention(1)
    latent_start()
    zlast(1)
    pack(1, (4, 5, 2, 3, 6, 7, 1, 0))
    reduce_second(3, 0)
    rows_arrive(0, 2)
    reduce_first(2, 0)
    build(True)
    latent_z()
    rows_arrive(1, 2)
    reduce_first(2, 1)
    reduce_second(2, 0)
    latent_x()
    rows_arrive(1, 1)
    reduce_first(1, 1)
    reduce_second(2, 1)
    rows_arrive(1, 3)
    reduce_first(3, 1)
    reduce_second(1, 1)
    reduce_last(2)
    swiglu_back(2)
    rows_arrive(1, 0)
    reduce_first(0, 1)
    reduce_second(3, 1)
    latent_y()
    reduce_last(1)
    swiglu_back(1)
    gather_forward(2)
    reduce_second(0, 1)
    reduce_last(3)
    swiglu_back(3)
    route_near(2)
    gather_forward(1)
    reduce_last(0)
    swiglu_back(0)
    route_far(2)
    gather_forward(3)
    route_near(1)
    route_far(1)
    gather_forward(0)
    latent_end()
    route_near(3)
    route_far(3)
    route_near(0)
    route_far(0)

    for s in (2, 1, 3, 0):
        for e in (0, 1):
            for dc in range(NC):
                if s or dc:
                    frm = plane(s, dc)
                    arrived(rrecv.at[frm, e], bidx(s, e, dc), dev(x, z, frm))

    def tokens(b):
        cols = pl.ds(pl.multiple_of(b * TOK, TOK), TOK)
        return tn(
            pick[:, :, cols].reshape(2 * NQ * SLOTS, TOK), rrecv[...].reshape(2 * NQ * SLOTS, WID)
        )

    def widx(way, step, piece):
        return OFF_ZRS + (way * 4 + step) * PIECES + piece

    def zsum_send(way, step, piece):
        rows = pl.ds(piece * PR, PR)
        to = zdev(1 if way == 0 else -1)
        send(zsend_v.at[way, step, rows], zrecv.at[way, step, rows], widx(way, step, piece), to)

    def zsum_got(way, step, piece):
        rows = pl.ds(piece * PR, PR)
        arrived(zrecv.at[way, step, rows], widx(way, step, piece), zdev(-1 if way == 0 else 1))
        return zrecv[way, step, rows].astype(F32)

    far = tokens((z + 4) % NZ).astype(BF)
    for way in (0, 1):
        for piece in pieces(way, 3):
            zsend_v[way, 0, pl.ds(piece * PR, PR)] = far[piece * PR : (piece + 1) * PR]
            zsum_send(way, 0, piece)
    for step in (1, 2, 3):
        accs = [tokens((z + 4 - step) % NZ), tokens((z + 4 + step) % NZ)]
        for piece in range(PIECES):
            for way in (0, 1):
                rows = accs[way][piece * PR : (piece + 1) * PR]
                if step > 1 or piece in pieces(way, 3):
                    rows = rows + zsum_got(way, step - 1, piece)
                zsend_v[way, step, pl.ds(piece * PR, PR)] = rows.astype(BF)
                zsum_send(way, step, piece)
    final = tokens(z)
    for piece in range(PIECES):
        rows = final[piece * PR : (piece + 1) * PR]
        for way in (0, 1):
            rows = rows + zsum_got(way, 3, piece)
        out_ref[pl.ds(piece * PR, PR)] = rows.astype(BF)

    for op in sends:
        op.wait_send()
    for s in range(NY):
        for e in (0, 1):
            for dc in range(NC):
                if s or dc:
                    copy(rsend.at[s, 0], rrecv.at[0, e], bidx(s, e, dc), dev(x, z, plane(-s, dc))).wait_send()


def settle(a_ref, b_ref, c_ref, x_ref, y_ref, z_ref):
    x_ref[...] = a_ref[...]
    y_ref[...] = b_ref[...]
    z_ref[...] = c_ref[...]


def per_device(
    moe_input, moe_grad, routes, gates, w_gate, w_up, w_down, queries, out_grad, positions, latents
):
    anywhere = pl.BlockSpec(memory_space=pl.ANY)
    vmem = pl.BlockSpec(memory_space=pltpu.VMEM)
    scratch = [
        pltpu.VMEM((2, NZ, TOK, WID), BF),
        pltpu.VMEM((NZ, 16, TOK), F32),
        pltpu.VMEM((2, WID, HID), BF),
        pltpu.VMEM((2, WID, HID), BF),
        pltpu.VMEM((2, HID, WID), BF),
        pltpu.VMEM((TOK, HEADS * LAT), BF),
        pltpu.VMEM((TOK, HEADS * VAL), BF),
        pltpu.VMEM((LAT, KEY_DEV), BF),
        pltpu.VMEM((NX, KEY_DEV, LAT), BF),
        pltpu.VMEM((NZ, 2 * NQ, TOK), F32),
        pltpu.VMEM((NZ, 2 * NQ, TOK), F32),
        pltpu.VMEM((2 * NQ, SLOTS, NZ * TOK), BF),
        pltpu.VMEM((2, NQ, 2, SLOTS, WID), BF),
        pltpu.VMEM((2, 2, NQ, SLOTS, WID), BF),
        pltpu.VMEM((NY, NX, 3, SLOTS, HID), BF),
        pltpu.VMEM((2, NY, 3, SLOTS, HID // 2), BF),
        pltpu.VMEM((2, NY, 3, SLOTS, HID), BF),
        pltpu.VMEM((NY, NX, 2, SLOTS, HID), BF),
        pltpu.VMEM((NY, NX, SLOTS, WID), BF),
        pltpu.VMEM((NQ, 2, SLOTS, WID), BF),
        pltpu.VMEM((2, 4, TOK, WID), BF),
        pltpu.VMEM((2, 4, TOK, WID), BF),
        pltpu.VMEM((KEYS, LAT), F32),
        pltpu.VMEM((NX, NC, 128, LAT), BF),
        pltpu.VMEM((NX, 128, LAT), BF),
        pltpu.VMEM((NX, NZ, 16, LAT), BF),
        pltpu.VMEM((NZ, NX, 16, LAT), BF),
        pltpu.VMEM((NX, 16, LAT), F32),
        pltpu.VMEM((NX, 16, LAT), F32),
        pltpu.VMEM((16, LAT), F32),
        pltpu.VMEM((NY, 16, LAT), F32),
        pltpu.SemaphoreType.DMA((N_SEM,)),
        pltpu.SemaphoreType.DMA((N_SEM,)),
        pltpu.SemaphoreType.DMA((9,)),
    ]
    out, q_grad, lat_grad = pl.pallas_call(
        body,
        out_shape=(
            jax.ShapeDtypeStruct((TOK, WID), BF),
            jax.ShapeDtypeStruct((TOK, HEADS * LAT), BF),
            jax.ShapeDtypeStruct((4, LAT), F32),
        ),
        in_specs=[anywhere] * 2 + [vmem] * 2 + [anywhere] * 5 + [vmem] + [anywhere],
        out_specs=(vmem, vmem, vmem),
        scratch_shapes=scratch,
        compiler_params=pltpu.CompilerParams(
            collective_id=0, has_side_effects=True, vmem_limit_bytes=63 * 2**20
        ),
    )(
        moe_input, moe_grad, routes.T, gates.T, w_gate, w_up, w_down, queries, out_grad,
        positions.reshape(1, TOK), latents.T,
    )
    return pl.pallas_call(
        settle,
        out_shape=[jax.ShapeDtypeStruct(v.shape, v.dtype) for v in (out, q_grad, lat_grad)],
        in_specs=[vmem] * 3,
        out_specs=[vmem] * 3,
    )(out, q_grad, lat_grad)


def solution(mesh):
    return jax.shard_map(
        per_device,
        mesh=mesh,
        in_specs=(
            P("exp", "ctx"),
            P("exp", "ctx"),
            P("exp", None),
            P("exp", None),
            P("exp", "ctx", None),
            P("exp", "ctx", None),
            P("exp", None, "ctx"),
            P("ctx", "exp"),
            P("ctx", "exp"),
            P("ctx"),
            P("ctx", None),
        ),
        out_specs=(P("exp", "ctx"), P("ctx", "exp"), P(("ctx", "exp"), None)),
        check_vma=False,
    )
```

```python
import jax
import jax.numpy as jnp
from jax import lax
from jax.experimental import pallas as pl
from jax.experimental.pallas import tpu as pltpu
from jax.sharding import PartitionSpec as P

SCORE_SCALE = 192.0 ** (-0.5)
MASKED = -1e30
MESH = pl.DeviceIdType.MESH
BF = jnp.bfloat16
F32 = jnp.float32

NX, NZ, NY, NC = 4, 8, 4, 2
NQ = NY * NC
TOK = 128
WID = 896
HID = 1024
CAP = 10
SLOTS = NZ * CAP
LAT = 576
VAL = 512
HEADS = 2
KEY_DEV = 256
KEYS = NX * KEY_DEV

PIECES = 4
N_ZAG = 2 * 2 * 4 * PIECES
N_META = 8
N_LAT = 4
N_PLANE = 16
N_BACK = 16
N_RS = 48
N_AG = 24
N_ZRS = 2 * 4 * PIECES
N_LG = 1 + 8 + 4 + 4

OFF_ZAG = 0
OFF_META = OFF_ZAG + N_ZAG
OFF_LAT = OFF_META + N_META
OFF_PLANE = OFF_LAT + N_LAT
OFF_BACK = OFF_PLANE + N_PLANE
OFF_RS = OFF_BACK + N_BACK
OFF_AG = OFF_RS + N_RS
OFF_ZRS = OFF_AG + N_AG
OFF_LG = OFF_ZRS + N_ZRS
N_SEM = OFF_LG + N_LG


def nn(a, b):
    return lax.dot_general(a, b, (((1,), (0,)), ((), ())), preferred_element_type=F32)


def nt(a, b):
    return lax.dot_general(a, b, (((1,), (1,)), ((), ())), preferred_element_type=F32)


def tn(a, b):
    return lax.dot_general(a, b, (((0,), (0,)), ((), ())), preferred_element_type=F32)


def body(
    in_hbm, grad_hbm, routes_ref, gates_ref, wg_hbm, wu_hbm, wd_hbm, q_hbm, og_hbm, pos_ref, lat_hbm,
    out_ref, qg_ref, lg_ref,
    tok, meta, wg, wu, wd, qv, ogv, latraw, lat, rank_s, gate_s, pick, ysend, yrecv,
    part, rs_mid, rs_in, bk, rsend, rrecv, zsend_v, zrecv,
    lacc, lout, lc_in, lz_out, lz_in, lx_out, lx_in, ly_out, ly_in,
    ssem, rsem, lsem,
):
    x = lax.axis_index("ctx")
    e_id = lax.axis_index("exp")
    z = e_id // NQ
    q = e_id % NQ
    y = q // NC
    c = q % NC

    def dev(xx, zz, qq):
        return (xx, zz * NQ + qq)

    def zdev(d):
        return dev(x, (z + d + NZ) % NZ, q)

    def xdev(d):
        return dev((x + d + NX) % NX, z, q)

    def plane(dy, dc):
        return ((y + dy + NY) % NY) * NC + (c + dc) % NC

    sends = []

    def copy(src, dst, idx, to):
        return pltpu.make_async_remote_copy(
            src_ref=src, dst_ref=dst, send_sem=ssem.at[idx], recv_sem=rsem.at[idx],
            device_id=to, device_id_type=MESH,
        )

    def send(src, dst, idx, to):
        op = copy(src, dst, idx, to)
        op.start()
        sends.append(op)

    def arrived(dst, idx, frm):
        copy(dst, dst, idx, frm).wait_recv()

    loads = []

    def load(src, dst):
        op = pltpu.make_async_copy(src, dst, lsem.at[len(loads)])
        op.start()
        loads.append(op)
        return op

    ld_in = load(in_hbm, tok.at[0, z])
    ld_lat = load(lat_hbm, latraw)
    ld_grad = load(grad_hbm, tok.at[1, z])
    ld_q = load(q_hbm, qv)
    ld_og = load(og_hbm, ogv)
    ld_wg = load(wg_hbm, wg)
    ld_wu = load(wu_hbm, wu)
    ld_wd = load(wd_hbm, wd)

    barrier = pltpu.get_barrier_semaphore()
    peers = [zdev(d) for d in range(1, NZ)]
    peers += [dev(x, z, plane(j // NC, j % NC)) for j in range(1, NQ)]
    peers += [xdev(d) for d in range(1, NX)]
    for peer in peers:
        pl.semaphore_signal(barrier, inc=1, device_id=peer, device_id_type=MESH)
    pl.semaphore_wait(barrier, len(peers))

    PR = TOK // PIECES

    def zidx(a, way, step, piece):
        return OFF_ZAG + ((a * 2 + way) * 4 + step) * PIECES + piece

    def pieces(way, step):
        if step < 3:
            return tuple(range(PIECES))
        return tuple(range(PIECES // 2)) if way == 0 else tuple(range(PIECES // 2, PIECES))

    def zpiece(a, way, dist, piece):
        b = (z - dist + NZ) % NZ if way == 0 else (z + dist) % NZ
        return tok.at[a, b, pl.ds(piece * PR, PR)]

    def zsend_piece(a, way, step, piece):
        blk = zpiece(a, way, step, piece)
        send(blk, blk, zidx(a, way, step, piece), zdev(1 if way == 0 else -1))

    def zsend(a):
        for piece in range(PIECES):
            for way in (0, 1):
                zsend_piece(a, way, 0, piece)

    def zforward(a, step):
        for piece in range(PIECES):
            for way in (0, 1):
                arrived(zpiece(a, way, step, piece), zidx(a, way, step - 1, piece), zdev(-1 if way == 0 else 1))
                if piece in pieces(way, step):
                    zsend_piece(a, way, step, piece)

    def zlast(a):
        for way in (0, 1):
            for piece in pieces(way, 3):
                arrived(zpiece(a, way, 4, piece), zidx(a, way, 3, piece), zdev(-1 if way == 0 else 1))

    ld_in.wait()
    zsend(0)
    meta[z, 0:8] = routes_ref[...].astype(F32)
    meta[z, 8:16] = gates_ref[...]
    for d in range(1, NZ):
        send(meta.at[z], meta.at[z], OFF_META + d, zdev(d))

    ld_lat.wait()
    new = lax.broadcasted_iota(jnp.int32, (KEY_DEV, KEY_DEV), 0)
    old = lax.broadcasted_iota(jnp.int32, (KEY_DEV, KEY_DEV), 1)
    src = ((new // 16) % 8) * 32 + ((new // 4) % 4) * 8 + (new // 128) * 4 + new % 4
    shuffle = jnp.where(src == old, 1.0, 0.0).astype(BF)
    lat[x] = nt(shuffle, latraw[...]).astype(BF)
    for d in range(1, NX):
        send(lat.at[x], lat.at[x], OFF_LAT + d, xdev(d))

    zforward(0, 1)
    zforward(0, 2)
    zforward(0, 3)
    ld_grad.wait()
    zsend(1)

    for d in range(1, NZ):
        b = (z - d + NZ) % NZ
        arrived(meta.at[b], OFF_META + d, dev(x, b, q))
    tri = jnp.where(
        lax.broadcasted_iota(jnp.int32, (TOK, TOK), 0) < lax.broadcasted_iota(jnp.int32, (TOK, TOK), 1),
        1.0, 0.0,
    ).astype(BF)
    names = (lax.broadcasted_iota(jnp.int32, (2 * NQ, TOK), 0) + z * (2 * NQ)).astype(F32)
    for b in range(NZ):
        member = jnp.zeros((2 * NQ, TOK), F32)
        gate = jnp.zeros((2 * NQ, TOK), F32)
        for k in range(8):
            hit = meta[b, k : k + 1, :] == names
            member = jnp.where(hit, 1.0, member)
            gate = jnp.where(hit, meta[b, 8 + k : 9 + k, :], gate)
        rank = nn(member.astype(BF), tri)
        rank_s[b] = jnp.where(member > 0.0, rank, -1.0)
        gate_s[b] = gate

    def slot_value(b):
        row = lax.broadcasted_iota(jnp.int32, (SLOTS, TOK), 0)
        return jnp.where(row % NZ == b, row // NZ, -5).astype(F32)

    def build(weighted):
        for b in range(NZ):
            value = slot_value(b)

            def one(i, carry):
                row = rank_s[b, pl.ds(i, 1), :]
                if weighted:
                    cell = jnp.where(row == value, gate_s[b, pl.ds(i, 1), :], 0.0)
                else:
                    cell = jnp.where(row == value, 1.0, 0.0)
                pick[i, :, b * TOK : (b + 1) * TOK] = cell.astype(BF)
                return carry

            lax.fori_loop(0, 2 * NQ, one, 0)

    build(False)

    col = lax.broadcasted_iota(jnp.int32, (TOK, KEYS), 1)
    key_pos = (
        (col // 256) * 256 + ((col // 16) % 8) * 32 + ((col // 4) % 4) * 8 + ((col // 128) % 2) * 4 + col % 4
    )

    eye = lax.broadcasted_iota(jnp.int32, (TOK, TOK), 0) == lax.broadcasted_iota(jnp.int32, (TOK, TOK), 1)
    row_pos = jnp.sum(jnp.where(eye, pos_ref[...].astype(F32), 0.0), axis=1, keepdims=True).astype(jnp.int32)

    def attention(h):
        keys = lat[...].reshape(KEYS, LAT)
        visible = key_pos <= row_pos
        qh = qv[:, h * LAT : (h + 1) * LAT]
        gh = ogv[:, h * VAL : (h + 1) * VAL]
        score = jnp.where(visible, nt(qh, keys) * SCORE_SCALE, MASKED)
        peak = jnp.max(score, axis=1, keepdims=True)
        raw = jnp.where(visible, jnp.exp(score - peak), 0.0)
        attend = raw / jnp.sum(raw, axis=1, keepdims=True)
        dots = nt(gh, keys[:, :VAL])
        row_dot = jnp.sum(attend * dots, axis=1, keepdims=True)
        grad = (attend * (dots - row_dot)).astype(BF)
        low = attend.astype(BF)
        qg_ref[:, h * LAT : (h + 1) * LAT] = (nn(grad, keys) * SCORE_SCALE).astype(BF)
        key_part = tn(grad, qh) * SCORE_SCALE
        val_part = tn(low, gh)
        if h == 0:
            lacc[...] = key_part
        else:
            lacc[...] += key_part
        lacc[:, :VAL] += val_part

    zlast(0)

    def pidx(a, j):
        return OFF_PLANE + a * NQ + j

    both = pl.ds(0, 2)

    def pack(a, offsets):
        for j in offsets:
            qq = plane(j // NC, j % NC)
            toks = tok[a].reshape(NZ * TOK, WID)
            rows = nn(pick[pl.ds(qq * 2, 2)].reshape(2 * SLOTS, NZ * TOK), toks).astype(BF)
            rows = rows.reshape(2, SLOTS, WID)
            if j == 0:
                yrecv[a, :, q] = rows
            else:
                ysend[a, qq] = rows
                send(ysend.at[a, qq], yrecv.at[a, both, q], pidx(a, j), dev(x, z, qq))

    def rows_arrive(a, s):
        for dc in range(NC):
            j = s * NC + dc
            if j:
                frm = plane(-s, dc)
                arrived(yrecv.at[a, both, frm], pidx(a, j), dev(x, z, frm))

    k_opp, k_right, k_left = (x + 2) % NX, (x + 1) % NX, (x + 3) % NX
    right, left = xdev(1), xdev(-1)
    low, high = pl.ds(0, HID // 2), pl.ds(HID // 2, HID // 2)
    every = pl.ds(0, SLOTS)
    UNITS = ((0, 2, ("gate", "up")), (2, 1, ("down",)))

    def partial(s, name, k):
        a, w = {"gate": (0, wg), "up": (0, wu), "down": (1, wd)}[name]
        e = k // NC
        rows = yrecv[a, e, plane(-s, 0) // NC * NC + k % NC]
        return nt(rows, w[e]) if name == "down" else nn(rows, w[e])

    def ridx(s, u, n):
        return OFF_RS + (s * 2 + u) * 6 + n

    def store_part(s, u, k):
        first, _, names_ = UNITS[u]
        for i, name in enumerate(names_):
            part[s, k, first + i] = partial(s, name, k).astype(BF)

    def reduce_first(s, u):
        first, n, _ = UNITS[u]
        rng = pl.ds(first, n)
        store_part(s, u, k_opp)
        send(part.at[s, k_opp, rng, every, low], rs_mid.at[0, s, rng], ridx(s, u, 0), right)
        send(part.at[s, k_opp, rng, every, high], rs_mid.at[1, s, rng], ridx(s, u, 1), left)
        store_part(s, u, k_right)
        send(part.at[s, k_right, rng, every, high], rs_in.at[0, s, rng, every, high], ridx(s, u, 2), right)
        store_part(s, u, k_left)
        send(part.at[s, k_left, rng, every, low], rs_in.at[1, s, rng, every, low], ridx(s, u, 3), left)

    def reduce_second(s, u):
        first, n, _ = UNITS[u]
        rng = pl.ds(first, n)
        for way, frm, to, k, cols in ((0, left, right, k_right, low), (1, right, left, k_left, high)):
            arrived(rs_mid.at[way, s, rng], ridx(s, u, way), frm)
            got = rs_mid[way, s, rng].astype(F32) + part[s, k, rng, :, cols].astype(F32)
            part[s, k, rng, :, cols] = got.astype(BF)
            send(part.at[s, k, rng, every, cols], rs_in.at[way, s, rng, every, cols], ridx(s, u, 4 + way), to)
        store_part(s, u, x)

    def reduce_last(s):
        for u in (0, 1):
            first, n, _ = UNITS[u]
            rng = pl.ds(first, n)
            arrived(rs_in.at[0, s, rng, every, high], ridx(s, u, 2), left)
            arrived(rs_in.at[1, s, rng, every, low], ridx(s, u, 3), right)
            arrived(rs_in.at[0, s, rng, every, low], ridx(s, u, 4), left)
            arrived(rs_in.at[1, s, rng, every, high], ridx(s, u, 5), right)

    def total(s, i):
        return part[s, x, i].astype(F32) + rs_in[0, s, i].astype(F32) + rs_in[1, s, i].astype(F32)

    def aidx(s, way, n):
        return OFF_AG + (s * 2 + way) * 3 + n

    def bk_cols(s, k, cols):
        return bk.at[s, k, both, every, cols]

    def swiglu_back(s):
        gate_pre, up_pre, hidden = (total(s, i) for i in range(3))
        sigma = jax.nn.sigmoid(gate_pre)
        bk[s, x, 0] = (hidden * up_pre * sigma * (1.0 + gate_pre * (1.0 - sigma))).astype(BF)
        bk[s, x, 1] = (hidden * gate_pre * sigma).astype(BF)
        t, b = bk_cols(s, x, low), bk_cols(s, x, high)
        send(t, t, aidx(s, 0, 0), right)
        send(b, b, aidx(s, 1, 0), left)
        send(b, b, aidx(s, 0, 1), right)
        send(t, t, aidx(s, 1, 1), left)

    def gather_forward(s):
        t, b = bk_cols(s, k_left, low), bk_cols(s, k_right, high)
        arrived(t, aidx(s, 0, 0), left)
        send(t, t, aidx(s, 0, 2), right)
        arrived(b, aidx(s, 1, 0), right)
        send(b, b, aidx(s, 1, 2), left)

    def gather_near(s):
        arrived(bk_cols(s, k_left, high), aidx(s, 0, 1), left)
        arrived(bk_cols(s, k_right, low), aidx(s, 1, 1), right)

    def gather_far(s):
        arrived(bk_cols(s, k_opp, low), aidx(s, 0, 2), left)
        arrived(bk_cols(s, k_opp, high), aidx(s, 1, 2), right)

    def bidx(s, e, dc):
        return OFF_BACK + (s * 2 + e) * NC + dc

    def route(s, k):
        e, cs = k // NC, k % NC
        dc = (cs + c) % NC
        qq = plane(-s, 0) // NC * NC + cs
        rows = (nt(bk[s, k, 0], wg[e]) + nt(bk[s, k, 1], wu[e])).astype(BF)
        if s:
            rsend[s, k] = rows
            copy(rsend.at[s, k], rrecv.at[q, e], bidx(s, e, dc), dev(x, z, qq)).start()
        else:

            @pl.when(dc != 0)
            def _():
                rsend[s, k] = rows
                copy(rsend.at[s, k], rrecv.at[q, e], bidx(s, e, 1), dev(x, z, plane(0, 1))).start()

            @pl.when(dc == 0)
            def _():
                rrecv[q, e] = rows

    def route_near(s):
        route(s, x)
        gather_near(s)
        route(s, k_left)
        route(s, k_right)

    def route_far(s):
        gather_far(s)
        route(s, k_opp)

    sib = plane(0, 1)

    def latent_start():
        lout[...] = lacc[...].astype(BF).reshape(NX, NC, 128, LAT)
        send(lout.at[:, 1 - c], lc_in, OFF_LG, dev(x, z, sib))

    def latent_z():
        arrived(lc_in, OFF_LG, dev(x, z, sib))
        mine = lacc[...].reshape(NX, NC, 128, LAT)
        summed = jnp.where(c == 0, mine[:, 0], mine[:, 1]) + lc_in[...].astype(F32)
        lacc[pl.ds(0, NX * 128)] = summed.reshape(NX * 128, LAT)
        lz_out[...] = summed.astype(BF).reshape(NX, NZ, 16, LAT)
        for d in range(1, NZ):
            send(lz_out.at[:, (z + d) % NZ], lz_in.at[d], OFF_LG + d, zdev(d))

    def latent_x():
        zsum = lacc[pl.ds(0, NX * 128)].reshape(NX, NZ, 16, LAT)
        zown = jnp.where(z == 0, zsum[:, 0], 0.0)
        for b in range(1, NZ):
            zown = zown + jnp.where(z == b, zsum[:, b], 0.0)
        for d in range(1, NZ):
            arrived(lz_in.at[d], OFF_LG + d, zdev(-d))
            zown = zown + lz_in[d].astype(F32)
        lx_out[...] = zown
        for d in range(1, NX):
            send(lx_out.at[(x + d) % NX], lx_in.at[d], OFF_LG + 8 + d, xdev(d))

    def latent_y():
        xsum = lx_out[x]
        for d in range(1, NX):
            arrived(lx_in.at[d], OFF_LG + 8 + d, xdev(-d))
            xsum = xsum + lx_in[d]
        ly_out[...] = xsum
        for d in range(1, NY):
            send(ly_out, ly_in.at[d], OFF_LG + 12 + d, dev(x, z, plane(d, 0)))

    def latent_end():
        ysum = ly_out[...]
        for d in range(1, NY):
            arrived(ly_in.at[d], OFF_LG + 12 + d, dev(x, z, plane(-d, 0)))
            ysum = ysum + ly_in[d]
        pick4 = jnp.where(y == 0, ysum[0:4], 0.0)
        for b in range(1, NY):
            pick4 = pick4 + jnp.where(y == b, ysum[4 * b : 4 * b + 4], 0.0)
        lg_ref[...] = pick4

    pack(0, (2, 6, 3, 7, 1, 0))
    ld_wg.wait()
    ld_wu.wait()
    ld_wd.wait()
    rows_arrive(0, 0)
    reduce_first(0, 0)
    pack(0, (4, 5))
    zforward(1, 1)
    ld_q.wait()
    ld_og.wait()
    for d in range(1, NX):
        arrived(lat.at[(x - d + NX) % NX], OFF_LAT + d, xdev(-d))
    attention(0)
    zforward(1, 2)
    reduce_second(0, 0)
    rows_arrive(0, 1)
    reduce_first(1, 0)
    rows_arrive(0, 3)
    reduce_first(3, 0)
    zforward(1, 3)
    reduce_second(1, 0)
    attention(1)
    latent_start()
    zlast(1)
    pack(1, (4, 5, 2, 3, 6, 7, 1, 0))
    reduce_second(3, 0)
    rows_arrive(0, 2)
    reduce_first(2, 0)
    build(True)
    latent_z()
    rows_arrive(1, 2)
    reduce_first(2, 1)
    reduce_second(2, 0)
    latent_x()
    rows_arrive(1, 1)
    reduce_first(1, 1)
    reduce_second(2, 1)
    rows_arrive(1, 3)
    reduce_first(3, 1)
    reduce_second(1, 1)
    reduce_last(2)
    swiglu_back(2)
    rows_arrive(1, 0)
    reduce_first(0, 1)
    reduce_second(3, 1)
    latent_y()
    reduce_last(1)
    swiglu_back(1)
    gather_forward(2)
    reduce_second(0, 1)
    reduce_last(3)
    swiglu_back(3)
    route_near(2)
    gather_forward(1)
    reduce_last(0)
    swiglu_back(0)
    route_far(2)
    gather_forward(3)
    route_near(1)
    route_far(1)
    gather_forward(0)
    latent_end()
    route_near(3)
    route_far(3)
    route_near(0)
    route_far(0)

    for s in (2, 1, 3, 0):
        for e in (0, 1):
            for dc in range(NC):
                if s or dc:
                    frm = plane(s, dc)
                    arrived(rrecv.at[frm, e], bidx(s, e, dc), dev(x, z, frm))

    def tokens(b):
        cols = pl.ds(pl.multiple_of(b * TOK, TOK), TOK)
        return tn(
            pick[:, :, cols].reshape(2 * NQ * SLOTS, TOK), rrecv[...].reshape(2 * NQ * SLOTS, WID)
        )

    def widx(way, step, piece):
        return OFF_ZRS + (way * 4 + step) * PIECES + piece

    def zsum_send(way, step, piece):
        rows = pl.ds(piece * PR, PR)
        to = zdev(1 if way == 0 else -1)
        send(zsend_v.at[way, step, rows], zrecv.at[way, step, rows], widx(way, step, piece), to)

    def zsum_got(way, step, piece):
        rows = pl.ds(piece * PR, PR)
        arrived(zrecv.at[way, step, rows], widx(way, step, piece), zdev(-1 if way == 0 else 1))
        return zrecv[way, step, rows].astype(F32)

    far = tokens((z + 4) % NZ).astype(BF)
    for way in (0, 1):
        for piece in pieces(way, 3):
            zsend_v[way, 0, pl.ds(piece * PR, PR)] = far[piece * PR : (piece + 1) * PR]
            zsum_send(way, 0, piece)
    for step in (1, 2, 3):
        accs = [tokens((z + 4 - step) % NZ), tokens((z + 4 + step) % NZ)]
        for turn in range(PIECES):
            for way in (0, 1):
                piece = (turn + (PIECES // 2 if way == 0 else 0)) % PIECES
                rows = accs[way][piece * PR : (piece + 1) * PR]
                if step > 1 or piece in pieces(way, 3):
                    rows = rows + zsum_got(way, step - 1, piece)
                zsend_v[way, step, pl.ds(piece * PR, PR)] = rows.astype(BF)
                zsum_send(way, step, piece)
    final = tokens(z)
    for turn in range(PIECES):
        piece = (turn + PIECES // 2) % PIECES
        rows = final[piece * PR : (piece + 1) * PR]
        for way in (0, 1):
            rows = rows + zsum_got(way, 3, piece)
        out_ref[pl.ds(piece * PR, PR)] = rows.astype(BF)

    for op in sends:
        op.wait_send()
    for s in range(NY):
        for e in (0, 1):
            for dc in range(NC):
                if s or dc:
                    copy(rsend.at[s, 0], rrecv.at[0, e], bidx(s, e, dc), dev(x, z, plane(-s, dc))).wait_send()


def settle(a_ref, b_ref, c_ref, x_ref, y_ref, z_ref):
    x_ref[...] = a_ref[...]
    y_ref[...] = b_ref[...]
    z_ref[...] = c_ref[...]


def per_device(
    moe_input, moe_grad, routes, gates, w_gate, w_up, w_down, queries, out_grad, positions, latents
):
    anywhere = pl.BlockSpec(memory_space=pl.ANY)
    vmem = pl.BlockSpec(memory_space=pltpu.VMEM)
    scratch = [
        pltpu.VMEM((2, NZ, TOK, WID), BF),
        pltpu.VMEM((NZ, 16, TOK), F32),
        pltpu.VMEM((2, WID, HID), BF),
        pltpu.VMEM((2, WID, HID), BF),
        pltpu.VMEM((2, HID, WID), BF),
        pltpu.VMEM((TOK, HEADS * LAT), BF),
        pltpu.VMEM((TOK, HEADS * VAL), BF),
        pltpu.VMEM((LAT, KEY_DEV), BF),
        pltpu.VMEM((NX, KEY_DEV, LAT), BF),
        pltpu.VMEM((NZ, 2 * NQ, TOK), F32),
        pltpu.VMEM((NZ, 2 * NQ, TOK), F32),
        pltpu.VMEM((2 * NQ, SLOTS, NZ * TOK), BF),
        pltpu.VMEM((2, NQ, 2, SLOTS, WID), BF),
        pltpu.VMEM((2, 2, NQ, SLOTS, WID), BF),
        pltpu.VMEM((NY, NX, 3, SLOTS, HID), BF),
        pltpu.VMEM((2, NY, 3, SLOTS, HID // 2), BF),
        pltpu.VMEM((2, NY, 3, SLOTS, HID), BF),
        pltpu.VMEM((NY, NX, 2, SLOTS, HID), BF),
        pltpu.VMEM((NY, NX, SLOTS, WID), BF),
        pltpu.VMEM((NQ, 2, SLOTS, WID), BF),
        pltpu.VMEM((2, 4, TOK, WID), BF),
        pltpu.VMEM((2, 4, TOK, WID), BF),
        pltpu.VMEM((KEYS, LAT), F32),
        pltpu.VMEM((NX, NC, 128, LAT), BF),
        pltpu.VMEM((NX, 128, LAT), BF),
        pltpu.VMEM((NX, NZ, 16, LAT), BF),
        pltpu.VMEM((NZ, NX, 16, LAT), BF),
        pltpu.VMEM((NX, 16, LAT), F32),
        pltpu.VMEM((NX, 16, LAT), F32),
        pltpu.VMEM((16, LAT), F32),
        pltpu.VMEM((NY, 16, LAT), F32),
        pltpu.SemaphoreType.DMA((N_SEM,)),
        pltpu.SemaphoreType.DMA((N_SEM,)),
        pltpu.SemaphoreType.DMA((9,)),
    ]
    out, q_grad, lat_grad = pl.pallas_call(
        body,
        out_shape=(
            jax.ShapeDtypeStruct((TOK, WID), BF),
            jax.ShapeDtypeStruct((TOK, HEADS * LAT), BF),
            jax.ShapeDtypeStruct((4, LAT), F32),
        ),
        in_specs=[anywhere] * 2 + [vmem] * 2 + [anywhere] * 5 + [vmem] + [anywhere],
        out_specs=(vmem, vmem, vmem),
        scratch_shapes=scratch,
        compiler_params=pltpu.CompilerParams(
            collective_id=0, has_side_effects=True, vmem_limit_bytes=63 * 2**20
        ),
    )(
        moe_input, moe_grad, routes.T, gates.T, w_gate, w_up, w_down, queries, out_grad,
        positions.reshape(1, TOK), latents.T,
    )
    return pl.pallas_call(
        settle,
        out_shape=[jax.ShapeDtypeStruct(v.shape, v.dtype) for v in (out, q_grad, lat_grad)],
        in_specs=[vmem] * 3,
        out_specs=[vmem] * 3,
    )(out, q_grad, lat_grad)


def solution(mesh):
    return jax.shard_map(
        per_device,
        mesh=mesh,
        in_specs=(
            P("exp", "ctx"),
            P("exp", "ctx"),
            P("exp", None),
            P("exp", None),
            P("exp", "ctx", None),
            P("exp", "ctx", None),
            P("exp", None, "ctx"),
            P("ctx", "exp"),
            P("ctx", "exp"),
            P("ctx"),
            P("ctx", None),
        ),
        out_specs=(P("exp", "ctx"), P("ctx", "exp"), P(("ctx", "exp"), None)),
        check_vma=False,
    )
```

```python
import jax
import jax.numpy as jnp
from jax import lax
from jax.experimental import pallas as pl
from jax.experimental.pallas import tpu as pltpu
from jax.sharding import PartitionSpec as P

SCORE_SCALE = 192.0 ** (-0.5)
MASKED = -1e30
MESH = pl.DeviceIdType.MESH
BF = jnp.bfloat16
F32 = jnp.float32

NX, NZ, NY, NC = 4, 8, 4, 2
NQ = NY * NC
TOK = 128
WID = 896
HID = 1024
CAP = 10
SLOTS = NZ * CAP
LAT = 576
VAL = 512
HEADS = 2
KEY_DEV = 256
KEYS = NX * KEY_DEV

PIECES = 4
N_ZAG = 2 * 2 * 4 * PIECES
N_META = 8
N_LAT = 4
N_PLANE = 16
N_BACK = 16
N_RS = 48
N_AG = 24
N_ZRS = 2 * 4 * PIECES
N_LG = 1 + 8 + 4 + 4

OFF_ZAG = 0
OFF_META = OFF_ZAG + N_ZAG
OFF_LAT = OFF_META + N_META
OFF_PLANE = OFF_LAT + N_LAT
OFF_BACK = OFF_PLANE + N_PLANE
OFF_RS = OFF_BACK + N_BACK
OFF_AG = OFF_RS + N_RS
OFF_ZRS = OFF_AG + N_AG
OFF_LG = OFF_ZRS + N_ZRS
N_SEM = OFF_LG + N_LG


def nn(a, b):
    return lax.dot_general(a, b, (((1,), (0,)), ((), ())), preferred_element_type=F32)


def nt(a, b):
    return lax.dot_general(a, b, (((1,), (1,)), ((), ())), preferred_element_type=F32)


def tn(a, b):
    return lax.dot_general(a, b, (((0,), (0,)), ((), ())), preferred_element_type=F32)


def body(
    in_hbm, grad_hbm, routes_ref, gates_ref, wg_hbm, wu_hbm, wd_hbm, q_hbm, og_hbm, pos_ref, lat_hbm,
    out_ref, qg_ref, lg_ref,
    tok, meta, wg, wu, wd, qv, ogv, latraw, lat, rank_s, gate_s, pick, ysend, yrecv,
    part, rs_mid, rs_in, bk, rsend, rrecv, zsend_v, zrecv,
    lacc, lout, lc_in, lz_out, lz_in, lx_out, lx_in, ly_out, ly_in,
    ssem, rsem, lsem,
):
    x = lax.axis_index("ctx")
    e_id = lax.axis_index("exp")
    z = e_id // NQ
    q = e_id % NQ
    y = q // NC
    c = q % NC

    def dev(xx, zz, qq):
        return (xx, zz * NQ + qq)

    def zdev(d):
        return dev(x, (z + d + NZ) % NZ, q)

    def xdev(d):
        return dev((x + d + NX) % NX, z, q)

    def plane(dy, dc):
        return ((y + dy + NY) % NY) * NC + (c + dc) % NC

    sends = []

    def copy(src, dst, idx, to):
        return pltpu.make_async_remote_copy(
            src_ref=src, dst_ref=dst, send_sem=ssem.at[idx], recv_sem=rsem.at[idx],
            device_id=to, device_id_type=MESH,
        )

    def send(src, dst, idx, to):
        op = copy(src, dst, idx, to)
        op.start()
        sends.append(op)

    def arrived(dst, idx, frm):
        copy(dst, dst, idx, frm).wait_recv()

    loads = []

    def load(src, dst):
        op = pltpu.make_async_copy(src, dst, lsem.at[len(loads)])
        op.start()
        loads.append(op)
        return op

    ld_in = load(in_hbm, tok.at[0, z])
    ld_lat = load(lat_hbm, latraw)
    ld_grad = load(grad_hbm, tok.at[1, z])
    ld_q = load(q_hbm, qv)
    ld_og = load(og_hbm, ogv)
    ld_wg = load(wg_hbm, wg)
    ld_wu = load(wu_hbm, wu)
    ld_wd = load(wd_hbm, wd)

    barrier = pltpu.get_barrier_semaphore()
    peers = [zdev(d) for d in range(1, NZ)]
    peers += [dev(x, z, plane(j // NC, j % NC)) for j in range(1, NQ)]
    peers += [xdev(d) for d in range(1, NX)]
    for peer in peers:
        pl.semaphore_signal(barrier, inc=1, device_id=peer, device_id_type=MESH)
    pl.semaphore_wait(barrier, len(peers))

    PR = TOK // PIECES

    def zidx(a, way, step, piece):
        return OFF_ZAG + ((a * 2 + way) * 4 + step) * PIECES + piece

    def pieces(way, step):
        if step < 3:
            return tuple(range(PIECES))
        return tuple(range(PIECES // 2)) if way == 0 else tuple(range(PIECES // 2, PIECES))

    def zpiece(a, way, dist, piece):
        b = (z - dist + NZ) % NZ if way == 0 else (z + dist) % NZ
        return tok.at[a, b, pl.ds(piece * PR, PR)]

    def zsend_piece(a, way, step, piece):
        blk = zpiece(a, way, step, piece)
        send(blk, blk, zidx(a, way, step, piece), zdev(1 if way == 0 else -1))

    def zsend(a):
        for piece in range(PIECES):
            for way in (0, 1):
                zsend_piece(a, way, 0, piece)

    def zforward(a, step):
        for piece in range(PIECES):
            for way in (0, 1):
                arrived(zpiece(a, way, step, piece), zidx(a, way, step - 1, piece), zdev(-1 if way == 0 else 1))
                if piece in pieces(way, step):
                    zsend_piece(a, way, step, piece)

    def zlast(a):
        for way in (0, 1):
            for piece in pieces(way, 3):
                arrived(zpiece(a, way, 4, piece), zidx(a, way, 3, piece), zdev(-1 if way == 0 else 1))

    ld_in.wait()
    zsend(0)
    meta[z, 0:8] = routes_ref[...].astype(F32)
    meta[z, 8:16] = gates_ref[...]
    for d in range(1, NZ):
        send(meta.at[z], meta.at[z], OFF_META + d, zdev(d))

    ld_lat.wait()
    new = lax.broadcasted_iota(jnp.int32, (KEY_DEV, KEY_DEV), 0)
    old = lax.broadcasted_iota(jnp.int32, (KEY_DEV, KEY_DEV), 1)
    src = ((new // 16) % 8) * 32 + ((new // 4) % 4) * 8 + (new // 128) * 4 + new % 4
    shuffle = jnp.where(src == old, 1.0, 0.0).astype(BF)
    lat[x] = nt(shuffle, latraw[...]).astype(BF)
    for d in range(1, NX):
        send(lat.at[x], lat.at[x], OFF_LAT + d, xdev(d))

    zforward(0, 1)

    for d in range(1, NZ):
        b = (z - d + NZ) % NZ
        arrived(meta.at[b], OFF_META + d, dev(x, b, q))
    tri = jnp.where(
        lax.broadcasted_iota(jnp.int32, (TOK, TOK), 0) < lax.broadcasted_iota(jnp.int32, (TOK, TOK), 1),
        1.0, 0.0,
    ).astype(BF)
    names = (lax.broadcasted_iota(jnp.int32, (2 * NQ, TOK), 0) + z * (2 * NQ)).astype(F32)
    for b in range(NZ):
        member = jnp.zeros((2 * NQ, TOK), F32)
        gate = jnp.zeros((2 * NQ, TOK), F32)
        for k in range(8):
            hit = meta[b, k : k + 1, :] == names
            member = jnp.where(hit, 1.0, member)
            gate = jnp.where(hit, meta[b, 8 + k : 9 + k, :], gate)
        rank = nn(member.astype(BF), tri)
        rank_s[b] = jnp.where(member > 0.0, rank, -1.0)
        gate_s[b] = gate

    def slot_value(b):
        row = lax.broadcasted_iota(jnp.int32, (SLOTS, TOK), 0)
        return jnp.where(row % NZ == b, row // NZ, -5).astype(F32)

    def build(weighted):
        for b in range(NZ):
            value = slot_value(b)

            def one(i, carry):
                row = rank_s[b, pl.ds(i, 1), :]
                if weighted:
                    cell = jnp.where(row == value, gate_s[b, pl.ds(i, 1), :], 0.0)
                else:
                    cell = jnp.where(row == value, 1.0, 0.0)
                pick[i, :, b * TOK : (b + 1) * TOK] = cell.astype(BF)
                return carry

            lax.fori_loop(0, 2 * NQ, one, 0)

    zforward(0, 2)
    build(False)
    zforward(0, 3)
    ld_grad.wait()
    zsend(1)

    col = lax.broadcasted_iota(jnp.int32, (TOK, KEYS), 1)
    key_pos = (
        (col // 256) * 256 + ((col // 16) % 8) * 32 + ((col // 4) % 4) * 8 + ((col // 128) % 2) * 4 + col % 4
    )

    eye = lax.broadcasted_iota(jnp.int32, (TOK, TOK), 0) == lax.broadcasted_iota(jnp.int32, (TOK, TOK), 1)
    row_pos = jnp.sum(jnp.where(eye, pos_ref[...].astype(F32), 0.0), axis=1, keepdims=True).astype(jnp.int32)

    def attention(h):
        keys = lat[...].reshape(KEYS, LAT)
        visible = key_pos <= row_pos
        qh = qv[:, h * LAT : (h + 1) * LAT]
        gh = ogv[:, h * VAL : (h + 1) * VAL]
        score = jnp.where(visible, nt(qh, keys) * SCORE_SCALE, MASKED)
        peak = jnp.max(score, axis=1, keepdims=True)
        raw = jnp.where(visible, jnp.exp(score - peak), 0.0)
        attend = raw / jnp.sum(raw, axis=1, keepdims=True)
        dots = nt(gh, keys[:, :VAL])
        row_dot = jnp.sum(attend * dots, axis=1, keepdims=True)
        grad = (attend * (dots - row_dot)).astype(BF)
        low = attend.astype(BF)
        qg_ref[:, h * LAT : (h + 1) * LAT] = (nn(grad, keys) * SCORE_SCALE).astype(BF)
        key_part = tn(grad, qh) * SCORE_SCALE
        val_part = tn(low, gh)
        if h == 0:
            lacc[...] = key_part
        else:
            lacc[...] += key_part
        lacc[:, :VAL] += val_part

    zlast(0)

    def pidx(a, j):
        return OFF_PLANE + a * NQ + j

    both = pl.ds(0, 2)

    def pack(a, offsets):
        for j in offsets:
            qq = plane(j // NC, j % NC)
            toks = tok[a].reshape(NZ * TOK, WID)
            rows = nn(pick[pl.ds(qq * 2, 2)].reshape(2 * SLOTS, NZ * TOK), toks).astype(BF)
            rows = rows.reshape(2, SLOTS, WID)
            if j == 0:
                yrecv[a, :, q] = rows
            else:
                ysend[a, qq] = rows
                send(ysend.at[a, qq], yrecv.at[a, both, q], pidx(a, j), dev(x, z, qq))

    def rows_arrive(a, s):
        for dc in range(NC):
            j = s * NC + dc
            if j:
                frm = plane(-s, dc)
                arrived(yrecv.at[a, both, frm], pidx(a, j), dev(x, z, frm))

    k_opp, k_right, k_left = (x + 2) % NX, (x + 1) % NX, (x + 3) % NX
    right, left = xdev(1), xdev(-1)
    low, high = pl.ds(0, HID // 2), pl.ds(HID // 2, HID // 2)
    every = pl.ds(0, SLOTS)
    UNITS = ((0, 2, ("gate", "up")), (2, 1, ("down",)))

    def partial(s, name, k):
        a, w = {"gate": (0, wg), "up": (0, wu), "down": (1, wd)}[name]
        e = k // NC
        rows = yrecv[a, e, plane(-s, 0) // NC * NC + k % NC]
        return nt(rows, w[e]) if name == "down" else nn(rows, w[e])

    def ridx(s, u, n):
        return OFF_RS + (s * 2 + u) * 6 + n

    def store_part(s, u, k):
        first, _, names_ = UNITS[u]
        for i, name in enumerate(names_):
            part[s, k, first + i] = partial(s, name, k).astype(BF)

    def reduce_first(s, u):
        first, n, _ = UNITS[u]
        rng = pl.ds(first, n)
        store_part(s, u, k_opp)
        send(part.at[s, k_opp, rng, every, low], rs_mid.at[0, s, rng], ridx(s, u, 0), right)
        send(part.at[s, k_opp, rng, every, high], rs_mid.at[1, s, rng], ridx(s, u, 1), left)
        store_part(s, u, k_right)
        send(part.at[s, k_right, rng, every, high], rs_in.at[0, s, rng, every, high], ridx(s, u, 2), right)
        store_part(s, u, k_left)
        send(part.at[s, k_left, rng, every, low], rs_in.at[1, s, rng, every, low], ridx(s, u, 3), left)

    def reduce_second(s, u):
        first, n, _ = UNITS[u]
        rng = pl.ds(first, n)
        for way, frm, to, k, cols in ((0, left, right, k_right, low), (1, right, left, k_left, high)):
            arrived(rs_mid.at[way, s, rng], ridx(s, u, way), frm)
            got = rs_mid[way, s, rng].astype(F32) + part[s, k, rng, :, cols].astype(F32)
            part[s, k, rng, :, cols] = got.astype(BF)
            send(part.at[s, k, rng, every, cols], rs_in.at[way, s, rng, every, cols], ridx(s, u, 4 + way), to)
        store_part(s, u, x)

    def reduce_last(s):
        for u in (0, 1):
            first, n, _ = UNITS[u]
            rng = pl.ds(first, n)
            arrived(rs_in.at[0, s, rng, every, high], ridx(s, u, 2), left)
            arrived(rs_in.at[1, s, rng, every, low], ridx(s, u, 3), right)
            arrived(rs_in.at[0, s, rng, every, low], ridx(s, u, 4), left)
            arrived(rs_in.at[1, s, rng, every, high], ridx(s, u, 5), right)

    def total(s, i):
        return part[s, x, i].astype(F32) + rs_in[0, s, i].astype(F32) + rs_in[1, s, i].astype(F32)

    def aidx(s, way, n):
        return OFF_AG + (s * 2 + way) * 3 + n

    def bk_cols(s, k, cols):
        return bk.at[s, k, both, every, cols]

    def swiglu_back(s):
        gate_pre, up_pre, hidden = (total(s, i) for i in range(3))
        sigma = jax.nn.sigmoid(gate_pre)
        bk[s, x, 0] = (hidden * up_pre * sigma * (1.0 + gate_pre * (1.0 - sigma))).astype(BF)
        bk[s, x, 1] = (hidden * gate_pre * sigma).astype(BF)
        t, b = bk_cols(s, x, low), bk_cols(s, x, high)
        send(t, t, aidx(s, 0, 0), right)
        send(b, b, aidx(s, 1, 0), left)
        send(b, b, aidx(s, 0, 1), right)
        send(t, t, aidx(s, 1, 1), left)

    def gather_forward(s):
        t, b = bk_cols(s, k_left, low), bk_cols(s, k_right, high)
        arrived(t, aidx(s, 0, 0), left)
        send(t, t, aidx(s, 0, 2), right)
        arrived(b, aidx(s, 1, 0), right)
        send(b, b, aidx(s, 1, 2), left)

    def gather_near(s):
        arrived(bk_cols(s, k_left, high), aidx(s, 0, 1), left)
        arrived(bk_cols(s, k_right, low), aidx(s, 1, 1), right)

    def gather_far(s):
        arrived(bk_cols(s, k_opp, low), aidx(s, 0, 2), left)
        arrived(bk_cols(s, k_opp, high), aidx(s, 1, 2), right)

    def bidx(s, e, dc):
        return OFF_BACK + (s * 2 + e) * NC + dc

    def route(s, k):
        e, cs = k // NC, k % NC
        dc = (cs + c) % NC
        qq = plane(-s, 0) // NC * NC + cs
        rows = (nt(bk[s, k, 0], wg[e]) + nt(bk[s, k, 1], wu[e])).astype(BF)
        if s:
            rsend[s, k] = rows
            copy(rsend.at[s, k], rrecv.at[q, e], bidx(s, e, dc), dev(x, z, qq)).start()
        else:

            @pl.when(dc != 0)
            def _():
                rsend[s, k] = rows
                copy(rsend.at[s, k], rrecv.at[q, e], bidx(s, e, 1), dev(x, z, plane(0, 1))).start()

            @pl.when(dc == 0)
            def _():
                rrecv[q, e] = rows

    def route_near(s):
        route(s, x)
        gather_near(s)
        route(s, k_left)
        route(s, k_right)

    def route_far(s):
        gather_far(s)
        route(s, k_opp)

    sib = plane(0, 1)

    def latent_start():
        lout[...] = lacc[...].astype(BF).reshape(NX, NC, 128, LAT)
        send(lout.at[:, 1 - c], lc_in, OFF_LG, dev(x, z, sib))

    def latent_z():
        arrived(lc_in, OFF_LG, dev(x, z, sib))
        mine = lacc[...].reshape(NX, NC, 128, LAT)
        summed = jnp.where(c == 0, mine[:, 0], mine[:, 1]) + lc_in[...].astype(F32)
        lacc[pl.ds(0, NX * 128)] = summed.reshape(NX * 128, LAT)
        lz_out[...] = summed.astype(BF).reshape(NX, NZ, 16, LAT)
        for d in range(1, NZ):
            send(lz_out.at[:, (z + d) % NZ], lz_in.at[d], OFF_LG + d, zdev(d))

    def latent_x():
        zsum = lacc[pl.ds(0, NX * 128)].reshape(NX, NZ, 16, LAT)
        zown = jnp.where(z == 0, zsum[:, 0], 0.0)
        for b in range(1, NZ):
            zown = zown + jnp.where(z == b, zsum[:, b], 0.0)
        for d in range(1, NZ):
            arrived(lz_in.at[d], OFF_LG + d, zdev(-d))
            zown = zown + lz_in[d].astype(F32)
        lx_out[...] = zown
        for d in range(1, NX):
            send(lx_out.at[(x + d) % NX], lx_in.at[d], OFF_LG + 8 + d, xdev(d))

    def latent_y():
        xsum = lx_out[x]
        for d in range(1, NX):
            arrived(lx_in.at[d], OFF_LG + 8 + d, xdev(-d))
            xsum = xsum + lx_in[d]
        ly_out[...] = xsum
        for d in range(1, NY):
            send(ly_out, ly_in.at[d], OFF_LG + 12 + d, dev(x, z, plane(d, 0)))

    def latent_end():
        ysum = ly_out[...]
        for d in range(1, NY):
            arrived(ly_in.at[d], OFF_LG + 12 + d, dev(x, z, plane(-d, 0)))
            ysum = ysum + ly_in[d]
        pick4 = jnp.where(y == 0, ysum[0:4], 0.0)
        for b in range(1, NY):
            pick4 = pick4 + jnp.where(y == b, ysum[4 * b : 4 * b + 4], 0.0)
        lg_ref[...] = pick4

    pack(0, (1, 0, 2, 3, 6, 7))
    ld_wg.wait()
    ld_wu.wait()
    ld_wd.wait()
    rows_arrive(0, 0)
    reduce_first(0, 0)
    pack(0, (4, 5))
    zforward(1, 1)
    ld_q.wait()
    ld_og.wait()
    for d in range(1, NX):
        arrived(lat.at[(x - d + NX) % NX], OFF_LAT + d, xdev(-d))
    attention(0)
    zforward(1, 2)
    reduce_second(0, 0)
    rows_arrive(0, 1)
    reduce_first(1, 0)
    rows_arrive(0, 3)
    reduce_first(3, 0)
    zforward(1, 3)
    reduce_second(1, 0)
    attention(1)
    latent_start()
    zlast(1)
    pack(1, (4, 5, 2, 3, 6, 7, 1, 0))
    reduce_second(3, 0)
    rows_arrive(0, 2)
    reduce_first(2, 0)
    build(True)
    latent_z()
    rows_arrive(1, 2)
    reduce_first(2, 1)
    reduce_second(2, 0)
    latent_x()
    rows_arrive(1, 1)
    reduce_first(1, 1)
    reduce_second(2, 1)
    rows_arrive(1, 3)
    reduce_first(3, 1)
    reduce_second(1, 1)
    reduce_last(2)
    swiglu_back(2)
    rows_arrive(1, 0)
    reduce_first(0, 1)
    reduce_second(3, 1)
    latent_y()
    reduce_last(1)
    swiglu_back(1)
    gather_forward(2)
    reduce_second(0, 1)
    reduce_last(3)
    swiglu_back(3)
    route_near(2)
    gather_forward(1)
    reduce_last(0)
    swiglu_back(0)
    route_far(2)
    gather_forward(3)
    route_near(1)
    route_far(1)
    gather_forward(0)
    latent_end()
    route_near(3)
    route_far(3)
    route_near(0)
    route_far(0)

    for s in (2, 1, 3, 0):
        for e in (0, 1):
            for dc in range(NC):
                if s or dc:
                    frm = plane(s, dc)
                    arrived(rrecv.at[frm, e], bidx(s, e, dc), dev(x, z, frm))

    def tokens(b):
        cols = pl.ds(pl.multiple_of(b * TOK, TOK), TOK)
        return tn(
            pick[:, :, cols].reshape(2 * NQ * SLOTS, TOK), rrecv[...].reshape(2 * NQ * SLOTS, WID)
        )

    def widx(way, step, piece):
        return OFF_ZRS + (way * 4 + step) * PIECES + piece

    def zsum_send(way, step, piece):
        rows = pl.ds(piece * PR, PR)
        to = zdev(1 if way == 0 else -1)
        send(zsend_v.at[way, step, rows], zrecv.at[way, step, rows], widx(way, step, piece), to)

    def zsum_got(way, step, piece):
        rows = pl.ds(piece * PR, PR)
        arrived(zrecv.at[way, step, rows], widx(way, step, piece), zdev(-1 if way == 0 else 1))
        return zrecv[way, step, rows].astype(F32)

    far = tokens((z + 4) % NZ).astype(BF)
    for way in (0, 1):
        for piece in pieces(way, 3):
            zsend_v[way, 0, pl.ds(piece * PR, PR)] = far[piece * PR : (piece + 1) * PR]
            zsum_send(way, 0, piece)
    for step in (1, 2, 3):
        accs = [tokens((z + 4 - step) % NZ), tokens((z + 4 + step) % NZ)]
        for turn in range(PIECES):
            for way in (0, 1):
                piece = (turn + (PIECES // 2 if way == 0 else 0)) % PIECES
                rows = accs[way][piece * PR : (piece + 1) * PR]
                if step > 1 or piece in pieces(way, 3):
                    rows = rows + zsum_got(way, step - 1, piece)
                zsend_v[way, step, pl.ds(piece * PR, PR)] = rows.astype(BF)
                zsum_send(way, step, piece)
    final = tokens(z)
    for turn in range(PIECES):
        piece = (turn + PIECES // 2) % PIECES
        rows = final[piece * PR : (piece + 1) * PR]
        for way in (0, 1):
            rows = rows + zsum_got(way, 3, piece)
        out_ref[pl.ds(piece * PR, PR)] = rows.astype(BF)

    for op in sends:
        op.wait_send()
    for s in range(NY):
        for e in (0, 1):
            for dc in range(NC):
                if s or dc:
                    copy(rsend.at[s, 0], rrecv.at[0, e], bidx(s, e, dc), dev(x, z, plane(-s, dc))).wait_send()


def settle(a_ref, b_ref, c_ref, x_ref, y_ref, z_ref):
    x_ref[...] = a_ref[...]
    y_ref[...] = b_ref[...]
    z_ref[...] = c_ref[...]


def per_device(
    moe_input, moe_grad, routes, gates, w_gate, w_up, w_down, queries, out_grad, positions, latents
):
    anywhere = pl.BlockSpec(memory_space=pl.ANY)
    vmem = pl.BlockSpec(memory_space=pltpu.VMEM)
    scratch = [
        pltpu.VMEM((2, NZ, TOK, WID), BF),
        pltpu.VMEM((NZ, 16, TOK), F32),
        pltpu.VMEM((2, WID, HID), BF),
        pltpu.VMEM((2, WID, HID), BF),
        pltpu.VMEM((2, HID, WID), BF),
        pltpu.VMEM((TOK, HEADS * LAT), BF),
        pltpu.VMEM((TOK, HEADS * VAL), BF),
        pltpu.VMEM((LAT, KEY_DEV), BF),
        pltpu.VMEM((NX, KEY_DEV, LAT), BF),
        pltpu.VMEM((NZ, 2 * NQ, TOK), F32),
        pltpu.VMEM((NZ, 2 * NQ, TOK), F32),
        pltpu.VMEM((2 * NQ, SLOTS, NZ * TOK), BF),
        pltpu.VMEM((2, NQ, 2, SLOTS, WID), BF),
        pltpu.VMEM((2, 2, NQ, SLOTS, WID), BF),
        pltpu.VMEM((NY, NX, 3, SLOTS, HID), BF),
        pltpu.VMEM((2, NY, 3, SLOTS, HID // 2), BF),
        pltpu.VMEM((2, NY, 3, SLOTS, HID), BF),
        pltpu.VMEM((NY, NX, 2, SLOTS, HID), BF),
        pltpu.VMEM((NY, NX, SLOTS, WID), BF),
        pltpu.VMEM((NQ, 2, SLOTS, WID), BF),
        pltpu.VMEM((2, 4, TOK, WID), BF),
        pltpu.VMEM((2, 4, TOK, WID), BF),
        pltpu.VMEM((KEYS, LAT), F32),
        pltpu.VMEM((NX, NC, 128, LAT), BF),
        pltpu.VMEM((NX, 128, LAT), BF),
        pltpu.VMEM((NX, NZ, 16, LAT), BF),
        pltpu.VMEM((NZ, NX, 16, LAT), BF),
        pltpu.VMEM((NX, 16, LAT), F32),
        pltpu.VMEM((NX, 16, LAT), F32),
        pltpu.VMEM((16, LAT), F32),
        pltpu.VMEM((NY, 16, LAT), F32),
        pltpu.SemaphoreType.DMA((N_SEM,)),
        pltpu.SemaphoreType.DMA((N_SEM,)),
        pltpu.SemaphoreType.DMA((9,)),
    ]
    out, q_grad, lat_grad = pl.pallas_call(
        body,
        out_shape=(
            jax.ShapeDtypeStruct((TOK, WID), BF),
            jax.ShapeDtypeStruct((TOK, HEADS * LAT), BF),
            jax.ShapeDtypeStruct((4, LAT), F32),
        ),
        in_specs=[anywhere] * 2 + [vmem] * 2 + [anywhere] * 5 + [vmem] + [anywhere],
        out_specs=(vmem, vmem, vmem),
        scratch_shapes=scratch,
        compiler_params=pltpu.CompilerParams(
            collective_id=0, has_side_effects=True, vmem_limit_bytes=63 * 2**20
        ),
    )(
        moe_input, moe_grad, routes.T, gates.T, w_gate, w_up, w_down, queries, out_grad,
        positions.reshape(1, TOK), latents.T,
    )
    return pl.pallas_call(
        settle,
        out_shape=[jax.ShapeDtypeStruct(v.shape, v.dtype) for v in (out, q_grad, lat_grad)],
        in_specs=[vmem] * 3,
        out_specs=[vmem] * 3,
    )(out, q_grad, lat_grad)


def solution(mesh):
    return jax.shard_map(
        per_device,
        mesh=mesh,
        in_specs=(
            P("exp", "ctx"),
            P("exp", "ctx"),
            P("exp", None),
            P("exp", None),
            P("exp", "ctx", None),
            P("exp", "ctx", None),
            P("exp", None, "ctx"),
            P("ctx", "exp"),
            P("ctx", "exp"),
            P("ctx"),
            P("ctx", None),
        ),
        out_specs=(P("exp", "ctx"), P("ctx", "exp"), P(("ctx", "exp"), None)),
        check_vma=False,
    )
```
